256 devices in a mesh: ens: 16 (over z_lo, x), space: 16 (over z_hi, y, core).
Axes of the slice: x: 4, y: 4, z: 8 (z_hi: 2, z_lo: 4; z = z_hi * 4 + z_lo), core: 2. Of those that a mesh axis runs over, the one named last changes fastest.
Arguments:
- latent: bfloat16 [16, 1024, 24576], P('ens', None, 'space'), may hold values from -6 to 6
- truth: bfloat16 [83, 24576], P(None, 'space'), may hold values from -6 to 6
- w_first: bfloat16 [1024, 1024], replicated, may hold values from -0.1875 to 0.1875
- w_second: bfloat16 [83, 1024], replicated, may hold values from -0.1875 to 0.1875
Outputs:
- loss: float32 [16], P('ens')
- field_grad: float32 [16, 83, 24576], P('ens', None, 'space')
- grad_first: float32 [1024, 1024], P(('ens', 'space'))
- grad_second: float32 [16, 83, 1024], P('ens')
The draws below stay inside these ranges and needn't reach their ends.
All inputs are finite; a program needn't handle non-finite values.
Results may differ from the reference program's by a relative error of at most 0.007.
Values may be sent and summed in bfloat16 or wider, within the bound.
No kernel may reach another device: no remote copies, remote signals or barrier semaphores. Data moves between devices by JAX's collectives and lax.ppermute only.
A program may use at most 64 MiB of HBM per device.

```python
import math
import jax
import jax.numpy as jnp
from jax import lax

C = 83
H = 1024
H2 = 1024
MEMBERS = 16
NPTS = 24576
N_ENS = 16


def shard_levels(rng, extent, split, smallest, high):
    gain, own = 1.0, jax.random.fold_in(rng, 6)
    for dim, blocks in split:
        draws = jnp.exp(jax.random.uniform(jax.random.fold_in(own, dim), (blocks,), jnp.float32, smallest / len(split), high / len(split)))
        gain = gain * jnp.repeat(draws, extent[dim] // blocks).reshape([-1 if axis == dim else 1 for axis in range(len(extent))])
    return gain


def normal_values(key, dims, width, bound, pieces=(), held_as=jnp.bfloat16):
    values = width * jax.random.normal(key, dims, jnp.float32)
    if pieces:
        values = values * shard_levels(key, dims, pieces, -0.22, 0.18)
    return jnp.clip(values, -bound, bound).astype(held_as)


def setup_inputs(seed: int = 0) -> dict:
    seeds = jax.random.split(jax.random.key(seed), 5)
    return {
        "latent": normal_values(seeds[0], (MEMBERS, H, NPTS), 1.0, 6.0, ((0, 16), (2, 16))),
        "truth": normal_values(seeds[1], (C, NPTS), 1.0, 6.0, ((1, 16),)),
        "w_first": normal_values(seeds[2], (H2, H), H ** -0.5, 0.1875),
        "w_second": normal_values(seeds[3], (C, H2), H2 ** -0.5, 0.1875),
    }


SMOOTH_SQ = 0.01

def forward_member(latent_one, w_first, w_second):
    pre_act = jnp.dot(w_first, latent_one, preferred_element_type=jnp.float32)
    hidden = (pre_act * jax.nn.sigmoid(pre_act)).astype(jnp.bfloat16)
    field = jnp.dot(w_second, hidden, preferred_element_type=jnp.float32).astype(jnp.bfloat16)
    return (pre_act, hidden, field)

def reference(latent, truth, w_first, w_second):
    members = N_ENS
    npoints = NPTS
    fields = lax.map(lambda single: forward_member(single, w_first, w_second)[2], latent)
    member_f = fields.astype(jnp.float32)
    truth_f = truth.astype(jnp.float32)
    position = jnp.arange(npoints).astype(jnp.float32)
    area = jnp.cos(math.pi * ((position + 0.5) / npoints - 0.5))
    self_term = jnp.sqrt(jnp.float32(SMOOTH_SQ))

    def pair_sums(current):
        spread = current[None] - member_f
        smooth_abs = jnp.sqrt(spread * spread + SMOOTH_SQ)
        return (lax.optimization_barrier(jnp.sum(smooth_abs, 0)) - self_term, lax.optimization_barrier(jnp.sum(spread / smooth_abs, 0)))
    pair_value, pair_slope = lax.map(pair_sums, member_f)
    gap = member_f - truth_f[None]
    gap_abs = jnp.sqrt(gap * gap + SMOOTH_SQ)
    pair_weight = 1.0 / (members * (members - 1))
    field_grad = area * (gap / gap_abs / members - pair_weight * pair_slope)
    loss = lax.optimization_barrier(jnp.sum(area * (gap_abs - pair_value / (2.0 * (members - 1))), axis=(1, 2))) / npoints

    def accumulate(carry, inputs):
        latent_one, grad_one = inputs
        pre_act, hidden, unused = forward_member(latent_one, w_first, w_second)
        grad_low = grad_one.astype(jnp.bfloat16)
        second = lax.dot_general(grad_low, hidden, (((1,), (1,)), ((), ())), preferred_element_type=jnp.float32)
        back = jnp.dot(w_second.T, grad_low, preferred_element_type=jnp.float32)
        sigma = jax.nn.sigmoid(pre_act)
        back_pre = (back * sigma * (1.0 + pre_act * (1.0 - sigma))).astype(jnp.bfloat16)
        first = carry + lax.dot_general(back_pre, latent_one, (((1,), (1,)), ((), ())), preferred_element_type=jnp.float32)
        return (first, second)
    first_total, seconds = lax.scan(accumulate, jnp.zeros((H2, H), jnp.float32), (latent, field_grad))
    scale = 1.0 / math.sqrt(members * npoints)
    return (loss, field_grad, first_total * scale, seconds * (members / math.sqrt(npoints)))
```

```python
import math

import jax
import jax.numpy as jnp
from jax import lax
from jax.experimental import pallas as pl
from jax.experimental.pallas import tpu as pltpu
from jax.sharding import Mesh
from jax.sharding import PartitionSpec as P

BF = jnp.bfloat16
F32 = jnp.float32
EPS = 0.01
C, H, H2 = 83, 1024, 1024
PTS = 1536
NPTS = 24576
MEMBERS = 16
GROUPS, USED, ROWS, LANES = 4, 21, 24, 384
PAD = GROUPS * ROWS
STEP = 512
HI, LO = 21, 22
VMEM = 60 * 1024 * 1024
NT = (((1,), (1,)), ((), ()))


def params(**more):
    return pltpu.CompilerParams(vmem_limit_bytes=VMEM, **more)


def whole(shape):
    return pl.BlockSpec(shape, lambda *_: (0,) * len(shape))


def forward_kernel(lat_ref, w1_ref, w2_ref, hid_ref, der_ref, blk_ref, w2t_ref, w2p, field):
    step = pl.program_id(0)

    @pl.when(step == 0)
    def _():
        w2 = jnp.concatenate([w2_ref[...].astype(F32), jnp.zeros((1, H2), F32)], 0)
        gap = jnp.zeros((ROWS - USED, H2), F32)
        parts = []
        for g in range(GROUPS):
            parts += [w2[g * USED : (g + 1) * USED], gap]
        padded = jnp.concatenate(parts, 0)
        w2p[...] = padded.astype(BF)
        tall = jnp.concatenate([padded, jnp.zeros((128 - PAD, H2), F32)], 0)
        w2t_ref[...] = tall.T.astype(BF)

    lat = lat_ref[0]
    total = jnp.zeros((PAD, STEP), F32)
    rows = 256
    for r in range(0, H2, rows):
        pre = jnp.dot(w1_ref[r : r + rows, :], lat, preferred_element_type=F32)
        sig = 0.5 * jnp.tanh(0.5 * pre) + 0.5
        act = pre * sig
        hid = act.astype(BF)
        hid_ref[r : r + rows, :] = hid
        der_ref[r : r + rows, :] = (sig + act * (1.0 - sig)).astype(BF)
        total += jnp.dot(w2p[:, r : r + rows], hid, preferred_element_type=F32)
    field[:, pl.ds(pl.multiple_of(step * STEP, STEP), STEP)] = total

    @pl.when(step == PTS // STEP - 1)
    def _():
        for g in range(GROUPS):
            for q in range(PTS // LANES):
                blk_ref[g * GROUPS + q] = field[
                    g * ROWS : (g + 1) * ROWS, q * LANES : (q + 1) * LANES
                ].astype(BF)


def forward(latent, w_first, w_second):
    return pl.pallas_call(
        forward_kernel,
        grid=(PTS // STEP,),
        in_specs=[
            pl.BlockSpec((1, H, STEP), lambda s: (0, 0, s)),
            whole((H2, H)),
            whole((C, H2)),
        ],
        out_specs=[
            pl.BlockSpec((H2, STEP), lambda s: (0, s)),
            pl.BlockSpec((H2, STEP), lambda s: (0, s)),
            whole((16, ROWS, LANES)),
            whole((H2, 128)),
        ],
        out_shape=[
            jax.ShapeDtypeStruct((H2, PTS), BF),
            jax.ShapeDtypeStruct((H2, PTS), BF),
            jax.ShapeDtypeStruct((16, ROWS, LANES), BF),
            jax.ShapeDtypeStruct((H2, 128), BF),
        ],
        scratch_shapes=[pltpu.VMEM((PAD, H2), BF), pltpu.VMEM((PAD, PTS), F32)],
        compiler_params=params(),
        name="forward",
    )(latent, w_first, w_second)


def pair_kernel(fields_ref, truth_ref, area_ref, out_ref, values, grads):
    lane_tiles = LANES // 128
    spots = (ROWS // 8) * lane_tiles
    for m in range(MEMBERS):
        block = fields_ref[m].astype(F32)
        for r in range(ROWS // 8):
            for l in range(lane_tiles):
                values[r * lane_tiles + l, m] = block[
                    r * 8 : (r + 1) * 8, l * 128 : (l + 1) * 128
                ]

    def spot(index, losses):
        v = [values[index, m] for m in range(MEMBERS)]
        truth = truth_ref[index]
        area = area_ref[index]
        value = [None] * MEMBERS
        slope = [None] * MEMBERS

        def add(store, m, term):
            store[m] = term if store[m] is None else store[m] + term

        for m in range(MEMBERS):
            for k in range(m + 1, MEMBERS):
                d = v[m] - v[k]
                square = d * d + EPS
                inverse = lax.rsqrt(square)
                s = square * inverse
                t = d * inverse
                add(value, m, s)
                add(value, k, s)
                add(slope, m, t)
                slope[k] = -t if slope[k] is None else slope[k] - t
        new = []
        for m in range(MEMBERS):
            gap = v[m] - truth
            square = gap * gap + EPS
            inverse = lax.rsqrt(square)
            grads[index, m] = area * (
                gap * inverse * (1.0 / MEMBERS)
                - slope[m] * (1.0 / (MEMBERS * (MEMBERS - 1)))
            )
            new.append(area * (square * inverse - value[m] * (1.0 / (2.0 * (MEMBERS - 1)))))
        return [a + b for a, b in zip(losses, new)]

    zero = [jnp.zeros((8, 128), F32) for _ in range(MEMBERS)]
    row = lax.broadcasted_iota(jnp.int32, (8, 128), 0)
    last = ROWS // 8 - 1
    for l in range(lane_tiles):
        losses = lax.fori_loop(
            0, ROWS // 8, lambda r, carry: spot(r * lane_tiles + l, carry), zero
        )
        for m in range(MEMBERS):
            loss = jnp.sum(losses[m], axis=0, keepdims=True)
            high = loss.astype(BF).astype(F32)
            low = loss - high
            at = last * lane_tiles + l
            kept = grads[at, m]
            grads[at, m] = jnp.where(
                row == HI - 8 * last, high, jnp.where(row == LO - 8 * last, low, kept)
            )
    for m in range(MEMBERS):
        out_ref[m] = jnp.concatenate(
            [
                jnp.concatenate([grads[r * lane_tiles + l, m] for l in range(lane_tiles)], 1)
                for r in range(ROWS // 8)
            ],
            0,
        ).astype(BF)


def pairs(fields, truth, area):
    spots = ROWS // 8 * (LANES // 128)
    return pl.pallas_call(
        pair_kernel,
        out_shape=jax.ShapeDtypeStruct((16, ROWS, LANES), BF),
        in_specs=[pl.BlockSpec(memory_space=pltpu.VMEM)] * 3,
        out_specs=pl.BlockSpec(memory_space=pltpu.VMEM),
        scratch_shapes=[
            pltpu.VMEM((spots, MEMBERS, 8, 128), F32),
            pltpu.VMEM((spots, MEMBERS, 8, 128), F32),
        ],
        compiler_params=params(),
        name="pairs",
    )(fields, truth, area)


def arrange(rows):
    out = []
    for x in range(4):
        for y in range(4):
            pick = [rows[x * 64 + zh * 32 + y * 8 : x * 64 + zh * 32 + y * 8 + 8] for zh in range(2)]
            out.append(jnp.concatenate(pick, 0))
    return out


def back_kernel(
    core_ref, blk_ref, hid_ref, der_ref, lat_ref, w2t_ref,
    grad_ref, bp_ref, send_ref, second_ref, low, first,
):
    step = pl.program_id(0)

    @pl.when(step == 0)
    def _():
        for q in range(PTS // LANES):
            cols = pl.ds(q * LANES, LANES)
            parts = [blk_ref[g * GROUPS + q].astype(F32) for g in range(GROUPS)]
            for g in range(GROUPS):
                used = min(USED, C - g * USED)
                grad_ref[0, g * USED : g * USED + used, cols] = parts[g][:used]
            low[:, cols] = jnp.concatenate(
                parts + [jnp.zeros((128 - PAD, LANES), F32)], 0
            ).astype(BF)

    low_now = low[:, pl.ds(pl.multiple_of(step * STEP, STEP), STEP)]
    back = jnp.dot(w2t_ref[...], low_now, preferred_element_type=F32)
    bp = (back * der_ref[...].astype(F32)).astype(BF)
    bp_ref[...] = bp
    second = lax.dot_general(low_now, hid_ref[...], NT, preferred_element_type=F32)[:PAD]
    part = lax.dot_general(bp, lat_ref[0], NT, preferred_element_type=F32)

    @pl.when(step == 0)
    def _():
        second_ref[...] = second
        first[...] = part

    @pl.when(step > 0)
    def _():
        second_ref[...] += second
        first[...] += part

    @pl.when(step == PTS // STEP - 1)
    def _():
        for z in range(4):
            for e, piece in enumerate(arrange(first[z * 256 : (z + 1) * 256, :])):
                send_ref[e, z * 16 : (z + 1) * 16, :] = piece.astype(BF)
        row = lax.broadcasted_iota(jnp.int32, (8, LANES), 0)
        total = jnp.zeros((1, LANES), F32)
        for e in range(16):
            block = blk_ref[e].astype(F32)
            total += block[HI : HI + 1] + block[LO : LO + 1]
        high = total.astype(BF).astype(F32)
        top = ROWS - 8
        second_ref[top:ROWS, :LANES] = jnp.where(
            row == HI - top, high, jnp.where(row == LO - top, total - high, second_ref[top:ROWS, :LANES])
        )


def backward(core, blocks, hidden, deriv, latent, w2t):
    half = H // 2
    return pl.pallas_call(
        back_kernel,
        grid_spec=pltpu.PrefetchScalarGridSpec(
            num_scalar_prefetch=1,
            grid=(PTS // STEP,),
            in_specs=[
                whole((16, ROWS, LANES)),
                pl.BlockSpec((H2, STEP), lambda s, c: (0, s)),
                pl.BlockSpec((H2, STEP), lambda s, c: (0, s)),
                pl.BlockSpec((1, half, STEP), lambda s, c: (0, 1 - c[0], s)),
                whole((H2, 128)),
            ],
            out_specs=[
                whole((1, C, PTS)),
                pl.BlockSpec((H2, STEP), lambda s, c: (0, s)),
                whole((16, 64, half)),
                whole((PAD, H2)),
            ],
            scratch_shapes=[pltpu.VMEM((128, PTS), BF), pltpu.VMEM((H2, half), F32)],
        ),
        out_shape=[
            jax.ShapeDtypeStruct((1, C, PTS), F32),
            jax.ShapeDtypeStruct((H2, PTS), BF),
            jax.ShapeDtypeStruct((16, 64, half), BF),
            jax.ShapeDtypeStruct((PAD, H2), F32),
        ],
        compiler_params=params(),
        name="backward",
    )(core, blocks, hidden, deriv, latent, w2t)


def own_kernel(core_ref, bp_ref, lat_ref, out_ref):
    part = lax.dot_general(bp_ref[...], lat_ref[0], NT, preferred_element_type=F32)
    for e, piece in enumerate(arrange(part)):
        out_ref[e] = piece


def own_half(core, bp, latent):
    half = H // 2
    return pl.pallas_call(
        own_kernel,
        grid_spec=pltpu.PrefetchScalarGridSpec(
            num_scalar_prefetch=1,
            grid=(4,),
            in_specs=[
                pl.BlockSpec((256, PTS), lambda z, c: (z, 0)),
                pl.BlockSpec((1, half, PTS), lambda z, c: (0, c[0], 0)),
            ],
            out_specs=pl.BlockSpec((16, 16, half), lambda z, c: (0, z, 0)),
        ),
        out_shape=jax.ShapeDtypeStruct((16, 64, half), F32),
        compiler_params=params(),
        cost_estimate=pl.CostEstimate(
            flops=2 * H2 * half * PTS, bytes_accessed=7 * 1024 * 1024, transcendentals=0
        ),
        name="own_half",
    )(core, bp, latent)


def swap(value, axis, by):
    size = lax.axis_size(axis)
    return lax.ppermute(value, axis, [(i, i ^ by) for i in range(size)])


def packed(total):
    row = lax.broadcasted_iota(jnp.int32, total.shape, 0)
    loss = total[HI : HI + 1] + total[LO : LO + 1]
    high = lax.reduce_precision(loss, 8, 7)
    return jnp.where(row == HI, high, jnp.where(row == LO, loss - high, total)).astype(BF)


def on_device(latent, truth, w_first, w_second):
    core = lax.axis_index("c").astype(jnp.int32)
    group, quarter = lax.axis_index("zl"), lax.axis_index("x")
    place = (lax.axis_index("zh") * 4 + lax.axis_index("y")) * 2 + lax.axis_index("c")

    hidden, deriv, blocks, w2t = forward(latent, w_first, w_second)

    position = (place * PTS + quarter * LANES + jnp.arange(LANES)).astype(F32)
    area = jnp.cos(math.pi * ((position + 0.5) / NPTS - 0.5))
    rows = jnp.arange(ROWS)
    valid = (rows < USED) & (group * USED + rows < C)
    area = jnp.where(valid[:, None], area[None], 0.0)
    truth_pad = jnp.pad(truth, ((0, GROUPS * USED + ROWS - USED - C), (0, 0)))
    truth_here = lax.dynamic_slice(truth_pad, (group * USED, quarter * LANES), (ROWS, LANES))

    def spots(value):
        value = value.reshape(ROWS // 8, 8, LANES // 128, 128)
        return value.transpose(0, 2, 1, 3).reshape(-1, 8, 128)

    area, truth_here = spots(area), spots(truth_here.astype(F32))

    gathered = lax.all_to_all(blocks, ("zl", "x"), 0, 0, tiled=True)
    grads = pairs(gathered, truth_here, area)
    grads = lax.all_to_all(grads, ("zl", "x"), 0, 0, tiled=True)

    field_grad, bp, send, second = backward(core[None], grads, hidden, deriv, latent, w2t)

    arrived = swap(send, "c", 1)
    own = own_half(core[None], bp, latent)
    first = (own + arrived.astype(F32)).astype(BF)

    first = lax.all_to_all(first, ("x", "y"), 0, 0, tiled=True)
    first = jnp.sum(first.astype(F32), 0).astype(BF).reshape(8, 8, H // 2)
    first = lax.all_to_all(first, ("zl", "zh"), 0, 0, tiled=True)
    first = jnp.sum(first.astype(F32), 0) * (1.0 / math.sqrt(MEMBERS * NPTS))
    low, high = first[:4], first[4:]
    mine = jnp.where(core == 0, low, high)
    other = swap(jnp.where(core == 0, high, low), "c", 1)
    first_out = jnp.concatenate(
        [jnp.where(core == 0, mine, other), jnp.where(core == 0, other, mine)], 1
    )

    total = packed(second)
    for axis, by in (("c", 1), ("y", 1), ("y", 2), ("zh", 1)):
        got = swap(total, axis, by)
        summed = total.astype(F32) + got.astype(F32)
        total = packed(summed)
    loss = (jnp.sum(summed[HI, :LANES] + summed[LO, :LANES]) / NPTS)[None]
    kept = summed.reshape(GROUPS, ROWS, H2)[:, :USED].reshape(GROUPS * USED, H2)[:C]
    second_out = (kept * (MEMBERS / math.sqrt(NPTS)))[None]
    return loss, field_grad, first_out, second_out


def solution(mesh):
    fine = Mesh(mesh.devices.reshape(4, 4, 2, 4, 2), ("zl", "x", "zh", "y", "c"))
    ens, space = ("zl", "x"), ("zh", "y", "c")
    in_specs = (P(ens, None, space), P(None, space), P(), P())
    out_specs = (P(ens), P(ens, None, space), P(ens + space, None), P(ens, None, None))
    return jax.shard_map(
        on_device, mesh=fine, in_specs=in_specs, out_specs=out_specs, check_vma=False
    )
```

```python
import functools
import math

import jax
import jax.numpy as jnp
from jax import lax
from jax.experimental import pallas as pl
from jax.experimental.pallas import tpu as pltpu
from jax.sharding import Mesh
from jax.sharding import PartitionSpec as P

BF = jnp.bfloat16
F32 = jnp.float32
EPS = 0.01
C, H, H2 = 83, 1024, 1024
PTS = 1536
NPTS = 24576
MEMBERS = 16
GROUPS, USED, ROWS, LANES = 4, 21, 24, 384
PAD = GROUPS * ROWS
WIDE = 512
HI, LO = 21, 22
FLOPS = 20_000_000_000
NT = (((1,), (1,)), ((), ()))
VM = pl.BlockSpec(memory_space=pltpu.VMEM)
HBM = pl.BlockSpec(memory_space=pltpu.HBM)
SCALAR = pl.BlockSpec(memory_space=pltpu.SMEM)


def params(mib=24):
    return pltpu.CompilerParams(vmem_limit_bytes=mib * 1024 * 1024)


def shape(dims, dtype=BF):
    return jax.ShapeDtypeStruct(dims, dtype)


def in_hbm(value):
    return pltpu.with_memory_space_constraint(value, pltpu.HBM)


def own_tiles(where_ref, all_truth_ref, truth_ref, area_ref):
    lane_tiles = LANES // 128
    group, quarter, place = where_ref[0], where_ref[1], where_ref[2]
    cols = pl.ds(pl.multiple_of(quarter * LANES, 128), LANES)
    all_truth = jnp.concatenate(
        [all_truth_ref[:, cols].astype(F32), jnp.zeros((GROUPS * USED + ROWS - USED - C, LANES), F32)], 0
    )
    truth_here = all_truth[:ROWS]
    for g in range(1, GROUPS):
        truth_here = jnp.where(group == g, all_truth[g * USED : g * USED + ROWS], truth_here)
    lane = lax.broadcasted_iota(jnp.int32, (ROWS, LANES), 1)
    row = lax.broadcasted_iota(jnp.int32, (ROWS, LANES), 0)
    position = (place * PTS + quarter * LANES + lane).astype(F32)
    area_here = jnp.cos(math.pi * ((position + 0.5) / NPTS - 0.5))
    area_here = jnp.where((row < USED) & (group * USED + row < C), area_here, 0.0)
    for r in range(ROWS // 8):
        for l in range(lane_tiles):
            tile = (slice(r * 8, (r + 1) * 8), slice(l * 128, (l + 1) * 128))
            truth_ref[r * lane_tiles + l] = truth_here[tile]
            area_ref[r * lane_tiles + l] = area_here[tile]


def forward_kernel(
    where_ref, lat_hbm, w1_hbm, w2_hbm, truth_hbm,
    hid_ref, der_ref, lat_ref, blk_ref, w2t_ref, truth_ref, area_ref,
    w1, w2_ref, all_truth, w2p, field, sems,
):
    halves, spans = 2, PTS // WIDE
    rows = H2 // halves
    w1_in = [
        pltpu.make_async_copy(
            w1_hbm.at[r * rows : (r + 1) * rows], w1.at[r * rows : (r + 1) * rows], sems.at[r]
        )
        for r in range(halves)
    ]
    lat_in = [
        pltpu.make_async_copy(
            lat_hbm.at[0, :, n * WIDE : (n + 1) * WIDE],
            lat_ref.at[:, n * WIDE : (n + 1) * WIDE],
            sems.at[halves + n],
        )
        for n in range(spans)
    ]
    w2_in = pltpu.make_async_copy(w2_hbm, w2_ref, sems.at[halves + spans])
    truth_in = pltpu.make_async_copy(truth_hbm, all_truth, sems.at[halves + spans + 1])
    for copy in [w2_in, truth_in, w1_in[0], lat_in[0]] + w1_in[1:] + lat_in[1:]:
        copy.start()
    w2_in.wait()
    w2 = jnp.concatenate([w2_ref[...].astype(F32), jnp.zeros((1, H2), F32)], 0)
    gap = jnp.zeros((ROWS - USED, H2), F32)
    parts = []
    for g in range(GROUPS):
        parts += [w2[g * USED : (g + 1) * USED], gap]
    padded = jnp.concatenate(parts, 0)
    w2p[...] = padded.astype(BF)
    w2t_ref[...] = jnp.concatenate([padded, jnp.zeros((128 - PAD, H2), F32)], 0).T.astype(BF)

    def decode(n):
        cols = slice(n * WIDE, (n + 1) * WIDE)
        field[:, cols] = jnp.dot(w2p[...], hid_ref[:, cols], preferred_element_type=F32)

    for n in range(spans):
        lat_in[n].wait()
        if n == 1:
            truth_in.wait()
            own_tiles(where_ref, all_truth, truth_ref, area_ref)
        cols = slice(n * WIDE, (n + 1) * WIDE)
        for r in range(halves):
            if n == 0:
                w1_in[r].wait()
            here = slice(r * rows, (r + 1) * rows)
            pre = jnp.dot(w1[here, :], lat_ref[:, cols], preferred_element_type=F32)
            sig = 0.5 * jnp.tanh(0.5 * pre) + 0.5
            act = pre * sig
            hid_ref[here, cols] = act.astype(BF)
            der_ref[here, cols] = (sig + act * (1.0 - sig)).astype(BF)
        if n > 0:
            decode(n - 1)
    decode(spans - 1)
    for g in range(GROUPS):
        for q in range(PTS // LANES):
            blk_ref[g * GROUPS + q] = field[
                g * ROWS : (g + 1) * ROWS, q * LANES : (q + 1) * LANES
            ].astype(BF)


def forward(where, latent, w_first, w_second, truth):
    spots = ROWS // 8 * (LANES // 128)
    return pl.pallas_call(
        forward_kernel,
        in_specs=[SCALAR, HBM, HBM, HBM, HBM],
        out_specs=[VM] * 7,
        out_shape=[
            shape((H2, PTS)),
            shape((H2, PTS)),
            shape((H, PTS)),
            shape((16, ROWS, LANES)),
            shape((H2, 128)),
            shape((spots, 8, 128), F32),
            shape((spots, 8, 128), F32),
        ],
        scratch_shapes=[
            pltpu.VMEM((H2, H), BF),
            pltpu.VMEM((C, H2), BF),
            pltpu.VMEM((C, PTS), BF),
            pltpu.VMEM((PAD, H2), BF),
            pltpu.VMEM((PAD, PTS), F32),
            pltpu.SemaphoreType.DMA((4 + PTS // WIDE,)),
        ],
        compiler_params=params(12),
        name="forward",
    )(where, in_hbm(latent), in_hbm(w_first), in_hbm(w_second), in_hbm(truth))


def pair_kernel(fields_ref, truth_ref, area_ref, out_ref, values, grads):
    lane_tiles = LANES // 128
    for m in range(MEMBERS):
        block = fields_ref[m].astype(F32)
        for r in range(ROWS // 8):
            for l in range(lane_tiles):
                values[r * lane_tiles + l, m] = block[
                    r * 8 : (r + 1) * 8, l * 128 : (l + 1) * 128
                ]

    def spot(index, losses):
        v = [values[index, m] for m in range(MEMBERS)]
        truth = truth_ref[index]
        area = area_ref[index]
        value = [None] * MEMBERS
        slope = [None] * MEMBERS

        def add(store, m, term):
            store[m] = term if store[m] is None else store[m] + term

        for m in range(MEMBERS):
            for k in range(m + 1, MEMBERS):
                d = v[m] - v[k]
                square = d * d + EPS
                inverse = lax.rsqrt(square)
                s = square * inverse
                t = d * inverse
                add(value, m, s)
                add(value, k, s)
                add(slope, m, t)
                slope[k] = -t if slope[k] is None else slope[k] - t
        new = []
        for m in range(MEMBERS):
            gap = v[m] - truth
            square = gap * gap + EPS
            inverse = lax.rsqrt(square)
            grads[index, m] = area * (
                gap * inverse * (1.0 / MEMBERS)
                - slope[m] * (1.0 / (MEMBERS * (MEMBERS - 1)))
            )
            new.append(area * (square * inverse - value[m] * (1.0 / (2.0 * (MEMBERS - 1)))))
        return [a + b for a, b in zip(losses, new)]

    zero = [jnp.zeros((8, 128), F32) for _ in range(MEMBERS)]
    row = lax.broadcasted_iota(jnp.int32, (8, 128), 0)
    last = ROWS // 8 - 1
    for l in range(lane_tiles):
        losses = lax.fori_loop(
            0, ROWS // 8, lambda r, carry: spot(r * lane_tiles + l, carry), zero
        )
        for m in range(MEMBERS):
            loss = jnp.sum(losses[m], axis=0, keepdims=True)
            high = loss.astype(BF).astype(F32)
            low = loss - high
            at = last * lane_tiles + l
            kept = grads[at, m]
            grads[at, m] = jnp.where(
                row == HI - 8 * last, high, jnp.where(row == LO - 8 * last, low, kept)
            )
    for m in range(MEMBERS):
        out_ref[m] = jnp.concatenate(
            [
                jnp.concatenate([grads[r * lane_tiles + l, m] for l in range(lane_tiles)], 1)
                for r in range(ROWS // 8)
            ],
            0,
        ).astype(BF)


def pairs(fields, truth, area):
    spots = ROWS // 8 * (LANES // 128)
    return pl.pallas_call(
        pair_kernel,
        out_shape=shape((16, ROWS, LANES)),
        in_specs=[VM] * 3,
        out_specs=VM,
        scratch_shapes=[
            pltpu.VMEM((spots, MEMBERS, 8, 128), F32),
            pltpu.VMEM((spots, MEMBERS, 8, 128), F32),
        ],
        compiler_params=params(6),
        name="pairs",
    )(fields, truth, area)


def arrange(rows):
    out = []
    for x in range(4):
        for y in range(4):
            pick = [rows[x * 64 + zh * 32 + y * 8 : x * 64 + zh * 32 + y * 8 + 8] for zh in range(2)]
            out.append(jnp.concatenate(pick, 0))
    return out


def half_of_first(bp_ref, lat_ref, half, out_ref):
    lat = lat_ref[pl.ds(pl.multiple_of(half * (H // 2), H // 2), H // 2), :]
    for z in range(4):
        part = lax.dot_general(
            bp_ref[z * 256 : (z + 1) * 256, :], lat, NT, preferred_element_type=F32
        )
        for e, piece in enumerate(arrange(part)):
            out_ref[e, z * 16 : (z + 1) * 16, :] = piece.astype(out_ref.dtype)


def back_kernel(
    core_ref, blk_ref, der_ref, lat_ref, w2t_ref, hid_ref,
    bp_ref, send_ref, keep2_ref, send2_ref, low, second,
):
    half = H // 2
    for q in range(PTS // LANES):
        parts = [blk_ref[g * GROUPS + q].astype(F32) for g in range(GROUPS)]
        parts.append(jnp.zeros((128 - PAD, LANES), F32))
        low[:, q * LANES : (q + 1) * LANES] = jnp.concatenate(parts, 0).astype(BF)
    for n in range(PTS // WIDE):
        cols = slice(n * WIDE, (n + 1) * WIDE)
        back = jnp.dot(w2t_ref[...], low[:, cols], preferred_element_type=F32)
        bp_ref[:, cols] = (back * der_ref[:, cols].astype(F32)).astype(BF)
    half_of_first(bp_ref, lat_ref, 1 - core_ref[0], send_ref)

    second[...] = lax.dot_general(low[:PAD, :], hid_ref[...], NT, preferred_element_type=F32)
    row = lax.broadcasted_iota(jnp.int32, (8, LANES), 0)
    total = jnp.zeros((1, LANES), F32)
    for e in range(16):
        block = blk_ref[e].astype(F32)
        total += block[HI : HI + 1] + block[LO : LO + 1]
    high = total.astype(BF).astype(F32)
    top = ROWS - 8
    second[top:ROWS, :LANES] = jnp.where(
        row == HI - top,
        high,
        jnp.where(row == LO - top, total - high, second[top:ROWS, :LANES]),
    )
    keep2_ref[...] = second[:, pl.ds(pl.multiple_of(core_ref[0] * half, half), half)]
    send2_ref[...] = second[:, pl.ds(pl.multiple_of((1 - core_ref[0]) * half, half), half)].astype(BF)


def backward(core, blocks, deriv, latent, w2t, hidden):
    return pl.pallas_call(
        back_kernel,
        in_specs=[SCALAR, VM, VM, VM, VM, VM],
        out_specs=[VM] * 4,
        out_shape=[
            shape((H2, PTS)),
            shape((16, 64, H // 2)),
            shape((PAD, H2 // 2), F32),
            shape((PAD, H2 // 2)),
        ],
        scratch_shapes=[pltpu.VMEM((128, PTS), BF), pltpu.VMEM((PAD, H2), F32)],
        compiler_params=params(12),
        name="backward",
    )(core, blocks, deriv, latent, w2t, hidden)


def own_kernel(core_ref, bp_ref, lat_ref, blk_ref, out_ref, grad_ref):
    half_of_first(bp_ref, lat_ref, core_ref[0], out_ref)
    for q in range(PTS // LANES):
        cols = slice(q * LANES, (q + 1) * LANES)
        for g in range(GROUPS):
            used = min(USED, C - g * USED)
            part = blk_ref[g * GROUPS + q].astype(F32)
            grad_ref[g * USED : g * USED + used, :, cols] = part[:used].reshape(used, 1, LANES)


def own_half(core, bp, latent, blocks):
    return pl.pallas_call(
        own_kernel,
        in_specs=[SCALAR, VM, VM, VM],
        out_specs=[VM] * 2,
        out_shape=[shape((16, 64, H // 2), F32), shape((C, 1, PTS), F32)],
        compiler_params=params(12),
        cost_estimate=pl.CostEstimate(
            flops=2 * H2 * (H // 2) * PTS, bytes_accessed=8 * 1024 * 1024, transcendentals=0
        ),
        name="own_half",
    )(core, bp, latent, blocks)


def sum_kernel(scale, parts_ref, out_ref):
    total = parts_ref[0].astype(F32)
    for e in range(1, parts_ref.shape[0]):
        total += parts_ref[e].astype(F32)
    out_ref[...] = (total * scale).astype(out_ref.dtype)


def sum_parts(parts, scale, dtype, flops):
    return pl.pallas_call(
        functools.partial(sum_kernel, scale),
        in_specs=[VM],
        out_specs=VM,
        out_shape=shape(parts.shape[1:], dtype),
        compiler_params=params(6),
        cost_estimate=pl.CostEstimate(flops=flops, bytes_accessed=parts.size * 2, transcendentals=0),
        name="sum_parts",
    )(parts)


def finish_kernel(core_ref, mine_ref, other_ref, second_ref, loss_ref):
    first_core = core_ref[0] == 0
    mine, other = mine_ref[...].astype(F32), other_ref[...].astype(F32)
    left, right = jnp.where(first_core, mine, other), jnp.where(first_core, other, mine)
    loss = left[HI : HI + 1, :LANES] + left[LO : LO + 1, :LANES]
    loss_ref[...] = jnp.sum(loss, axis=1, keepdims=True) / NPTS
    scale = MEMBERS / math.sqrt(NPTS)
    for g in range(GROUPS):
        used = min(USED, C - g * USED)
        for cols, part in ((slice(0, H2 // 2), left), (slice(H2 // 2, H2), right)):
            rows = part[g * ROWS : g * ROWS + used] * scale
            second_ref[g * USED : g * USED + used, :, cols] = rows.reshape(used, 1, H2 // 2)


def finish(core, mine, other):
    return pl.pallas_call(
        finish_kernel,
        in_specs=[SCALAR, VM, VM],
        out_specs=[VM, VM],
        out_shape=[shape((C, 1, H2), F32), shape((1, 1), F32)],
        compiler_params=params(6),
        name="finish",
    )(core, mine, other)


def swap(value, axis, by):
    size = lax.axis_size(axis)
    return lax.ppermute(value, axis, [(i, i ^ by) for i in range(size)])


def turn(value, axis, by):
    size = lax.axis_size(axis)
    return lax.ppermute(value, axis, [(i, (i + by) % size) for i in range(size)])


def packed(total):
    row = lax.broadcasted_iota(jnp.int32, total.shape, 0)
    loss = total[HI : HI + 1] + total[LO : LO + 1]
    high = lax.reduce_precision(loss, 8, 7)
    return jnp.where(row == HI, high, jnp.where(row == LO, loss - high, total)).astype(BF)


def on_device(latent, truth, w_first, w_second):
    core = lax.axis_index("c").astype(jnp.int32)
    group, quarter = lax.axis_index("zl"), lax.axis_index("x")
    place = (lax.axis_index("zh") * 4 + lax.axis_index("y")) * 2 + lax.axis_index("c")
    where = jnp.stack([group, quarter, place]).astype(jnp.int32)
    latent, where, core = lax.optimization_barrier((latent, where, core[None]))

    hidden, deriv, kept_latent, blocks, w2t, truth_here, area = forward(
        where, latent, w_first, w_second, truth
    )

    gathered = lax.all_to_all(blocks, ("zl", "x"), 0, 0, tiled=True)
    grads = pairs(gathered, truth_here, area)
    grads = lax.all_to_all(grads, ("zl", "x"), 0, 0, tiled=True)

    bp, send, keep2, send2 = backward(core, grads, deriv, kept_latent, w2t, hidden)
    arrived, arrived2 = swap(send, "c", 1), swap(send2, "c", 1)
    own, field_grad = own_half(core, bp, kept_latent, grads)
    first = (own + arrived.astype(F32)).astype(BF)
    total = packed(keep2 + arrived2.astype(F32))
    first, total = lax.optimization_barrier((first, total))

    total = packed(total.astype(F32) + swap(total, "zh", 1).astype(F32))
    first = lax.all_to_all(first, ("x", "y"), 0, 0, tiled=True)
    first = sum_parts(first, 1.0, BF, FLOPS).reshape(8, 8, H // 2)
    first, total = lax.optimization_barrier((first, total))
    ring = [turn(total, "y", by).astype(F32) for by in (1, 2, 3)]
    total = packed((total.astype(F32) + ring[1]) + (ring[0] + ring[2]))
    other2 = swap(total, "c", 1)
    first = lax.all_to_all(first, ("zl", "zh"), 0, 0, tiled=True)
    first, total, other2 = lax.optimization_barrier((first, total, other2))
    first = sum_parts(first, 1.0 / math.sqrt(MEMBERS * NPTS), F32, FLOPS)
    upper, under = first[:4], first[4:]
    mine = jnp.where(core[0] == 0, upper, under)
    other = swap(jnp.where(core[0] == 0, under, upper), "c", 1)
    first_out = jnp.concatenate(
        [jnp.where(core[0] == 0, mine, other), jnp.where(core[0] == 0, other, mine)], 1
    )
    second_out, loss = finish(core, total, other2)
    return loss[0], field_grad.transpose(1, 0, 2), first_out, second_out.transpose(1, 0, 2)


def solution(mesh):
    fine = Mesh(mesh.devices.reshape(4, 4, 2, 4, 2), ("zl", "x", "zh", "y", "c"))
    ens, space = ("zl", "x"), ("zh", "y", "c")
    in_specs = (P(ens, None, space), P(None, space), P(), P())
    out_specs = (P(ens), P(ens, None, space), P(ens + space, None), P(ens, None, None))
    return jax.shard_map(
        on_device, mesh=fine, in_specs=in_specs, out_specs=out_specs, check_vma=False
    )
```

```python
import functools
import math

import jax
import jax.numpy as jnp
from jax import lax
from jax.experimental import pallas as pl
from jax.experimental.pallas import tpu as pltpu
from jax.sharding import Mesh
from jax.sharding import PartitionSpec as P

BF = jnp.bfloat16
F32 = jnp.float32
EPS = 0.01
C, H, H2 = 83, 1024, 1024
PTS = 1536
NPTS = 24576
MEMBERS = 16
GROUPS, USED, ROWS, LANES = 4, 21, 24, 384
PAD = GROUPS * ROWS
WIDE = 512
HI, LO = 21, 22
FLOPS = 20_000_000_000
NT = (((1,), (1,)), ((), ()))
VM = pl.BlockSpec(memory_space=pltpu.VMEM)
HBM = pl.BlockSpec(memory_space=pltpu.HBM)
SCALAR = pl.BlockSpec(memory_space=pltpu.SMEM)


def params(mib=24):
    return pltpu.CompilerParams(vmem_limit_bytes=mib * 1024 * 1024)


def shape(dims, dtype=BF):
    return jax.ShapeDtypeStruct(dims, dtype)


def in_hbm(value):
    return pltpu.with_memory_space_constraint(value, pltpu.HBM)


def own_tiles(where_ref, all_truth_ref, truth_ref, area_ref):
    lane_tiles = LANES // 128
    group, quarter, place = where_ref[0], where_ref[1], where_ref[2]
    cols = pl.ds(pl.multiple_of(quarter * LANES, 128), LANES)
    all_truth = jnp.concatenate(
        [all_truth_ref[:, cols].astype(F32), jnp.zeros((GROUPS * USED + ROWS - USED - C, LANES), F32)], 0
    )
    truth_here = all_truth[:ROWS]
    for g in range(1, GROUPS):
        truth_here = jnp.where(group == g, all_truth[g * USED : g * USED + ROWS], truth_here)
    lane = lax.broadcasted_iota(jnp.int32, (ROWS, LANES), 1)
    row = lax.broadcasted_iota(jnp.int32, (ROWS, LANES), 0)
    position = (place * PTS + quarter * LANES + lane).astype(F32)
    area_here = jnp.cos(math.pi * ((position + 0.5) / NPTS - 0.5))
    area_here = jnp.where((row < USED) & (group * USED + row < C), area_here, 0.0)
    for r in range(ROWS // 8):
        for l in range(lane_tiles):
            tile = (slice(r * 8, (r + 1) * 8), slice(l * 128, (l + 1) * 128))
            truth_ref[r * lane_tiles + l] = truth_here[tile]
            area_ref[r * lane_tiles + l] = area_here[tile]


def forward_kernel(
    where_ref, lat_hbm, w1_hbm, w2_hbm, truth_hbm,
    hid_ref, der_ref, lat_ref, blk_ref, w2t_ref, truth_ref, area_ref,
    w1, w2_ref, all_truth, w2p, field, sems,
):
    halves, spans = 2, PTS // WIDE
    rows = H2 // halves
    w1_in = [
        pltpu.make_async_copy(
            w1_hbm.at[r * rows : (r + 1) * rows], w1.at[r * rows : (r + 1) * rows], sems.at[r]
        )
        for r in range(halves)
    ]
    lat_in = [
        pltpu.make_async_copy(
            lat_hbm.at[0, :, n * WIDE : (n + 1) * WIDE],
            lat_ref.at[:, n * WIDE : (n + 1) * WIDE],
            sems.at[halves + n],
        )
        for n in range(spans)
    ]
    w2_in = pltpu.make_async_copy(w2_hbm, w2_ref, sems.at[halves + spans])
    truth_in = pltpu.make_async_copy(truth_hbm, all_truth, sems.at[halves + spans + 1])
    for copy in [w2_in, truth_in, w1_in[0], lat_in[0]] + w1_in[1:] + lat_in[1:]:
        copy.start()
    w2_in.wait()
    w2 = jnp.concatenate([w2_ref[...].astype(F32), jnp.zeros((1, H2), F32)], 0)
    gap = jnp.zeros((ROWS - USED, H2), F32)
    parts = []
    for g in range(GROUPS):
        parts += [w2[g * USED : (g + 1) * USED], gap]
    padded = jnp.concatenate(parts, 0)
    w2p[...] = padded.astype(BF)
    w2t_ref[...] = (0.5 * jnp.concatenate([padded, jnp.zeros((128 - PAD, H2), F32)], 0)).T.astype(BF)

    def decode(n):
        cols = slice(n * WIDE, (n + 1) * WIDE)
        field[:, cols] = jnp.dot(w2p[...], hid_ref[:, cols], preferred_element_type=F32)

    def gate(pre, here, cols):
        half = 0.5 * pre
        t = jnp.tanh(half)
        twice = 1.0 + t
        act = half * twice
        hid_ref[here, cols] = act.astype(BF)
        der_ref[here, cols] = (twice + act * (1.0 - t)).astype(BF)

    held = None
    for n in range(spans):
        if n == 0:
            lat_in[0].wait()
        if n == 1:
            truth_in.wait()
            for copy in lat_in[1:]:
                copy.wait()
            own_tiles(where_ref, all_truth, truth_ref, area_ref)
        cols = slice(n * WIDE, (n + 1) * WIDE)
        for r in range(0, H2, 128):
            if n == 0 and r % rows == 0:
                w1_in[r // rows].wait()
            here = slice(r, r + 128)
            pre = jnp.dot(w1[here, :], lat_ref[:, cols], preferred_element_type=F32)
            if held is not None:
                gate(*held)
            held = (pre, here, cols)
        if n > 0:
            decode(n - 1)
    gate(*held)
    decode(spans - 1)
    for g in range(GROUPS):
        for q in range(PTS // LANES):
            blk_ref[g * GROUPS + q] = field[
                g * ROWS : (g + 1) * ROWS, q * LANES : (q + 1) * LANES
            ].astype(BF)


def forward(where, latent, w_first, w_second, truth):
    spots = ROWS // 8 * (LANES // 128)
    return pl.pallas_call(
        forward_kernel,
        in_specs=[SCALAR, HBM, HBM, HBM, HBM],
        out_specs=[VM] * 7,
        out_shape=[
            shape((H2, PTS)),
            shape((H2, PTS)),
            shape((H, PTS)),
            shape((16, ROWS, LANES)),
            shape((H2, 128)),
            shape((spots, 8, 128), F32),
            shape((spots, 8, 128), F32),
        ],
        scratch_shapes=[
            pltpu.VMEM((H2, H), BF),
            pltpu.VMEM((C, H2), BF),
            pltpu.VMEM((C, PTS), BF),
            pltpu.VMEM((PAD, H2), BF),
            pltpu.VMEM((PAD, PTS), F32),
            pltpu.SemaphoreType.DMA((4 + PTS // WIDE,)),
        ],
        compiler_params=params(12),
        name="forward",
    )(where, in_hbm(latent), in_hbm(w_first), in_hbm(w_second), in_hbm(truth))


def pair_kernel(fields_ref, truth_ref, area_ref, out_ref, values, grads):
    lane_tiles = LANES // 128
    for m in range(MEMBERS):
        block = fields_ref[m].astype(F32)
        for r in range(ROWS // 8):
            for l in range(lane_tiles):
                values[r * lane_tiles + l, m] = block[
                    r * 8 : (r + 1) * 8, l * 128 : (l + 1) * 128
                ]

    def spot(index, losses):
        v = [values[index, m] for m in range(MEMBERS)]
        truth = truth_ref[index]
        area = area_ref[index]
        value = [None] * MEMBERS
        slope = [None] * MEMBERS

        def add(store, m, term):
            store[m] = term if store[m] is None else store[m] + term

        for m in range(MEMBERS):
            for k in range(m + 1, MEMBERS):
                d = v[m] - v[k]
                square = d * d + EPS
                inverse = lax.rsqrt(square)
                s = square * inverse
                t = d * inverse
                add(value, m, s)
                add(value, k, s)
                add(slope, m, t)
                slope[k] = -t if slope[k] is None else slope[k] - t
        new = []
        for m in range(MEMBERS):
            gap = v[m] - truth
            square = gap * gap + EPS
            inverse = lax.rsqrt(square)
            grads[index, m] = area * (
                gap * inverse * (1.0 / MEMBERS)
                - slope[m] * (1.0 / (MEMBERS * (MEMBERS - 1)))
            )
            new.append(area * (square * inverse - value[m] * (1.0 / (2.0 * (MEMBERS - 1)))))
        return [a + b for a, b in zip(losses, new)]

    zero = [jnp.zeros((8, 128), F32) for _ in range(MEMBERS)]
    row = lax.broadcasted_iota(jnp.int32, (8, 128), 0)
    last = ROWS // 8 - 1
    for l in range(lane_tiles):
        losses = lax.fori_loop(
            0, ROWS // 8, lambda r, carry: spot(r * lane_tiles + l, carry), zero
        )
        for m in range(MEMBERS):
            loss = jnp.sum(losses[m], axis=0, keepdims=True)
            high = loss.astype(BF).astype(F32)
            low = loss - high
            at = last * lane_tiles + l
            kept = grads[at, m]
            grads[at, m] = jnp.where(
                row == HI - 8 * last, high, jnp.where(row == LO - 8 * last, low, kept)
            )
    for m in range(MEMBERS):
        out_ref[m] = jnp.concatenate(
            [
                jnp.concatenate([grads[r * lane_tiles + l, m] for l in range(lane_tiles)], 1)
                for r in range(ROWS // 8)
            ],
            0,
        ).astype(BF)


def pairs(fields, truth, area):
    spots = ROWS // 8 * (LANES // 128)
    return pl.pallas_call(
        pair_kernel,
        out_shape=shape((16, ROWS, LANES)),
        in_specs=[VM] * 3,
        out_specs=VM,
        scratch_shapes=[
            pltpu.VMEM((spots, MEMBERS, 8, 128), F32),
            pltpu.VMEM((spots, MEMBERS, 8, 128), F32),
        ],
        compiler_params=params(6),
        name="pairs",
    )(fields, truth, area)


def arrange(rows):
    out = []
    for x in range(4):
        for y in range(4):
            pick = [rows[x * 64 + zh * 32 + y * 8 : x * 64 + zh * 32 + y * 8 + 8] for zh in range(2)]
            out.append(jnp.concatenate(pick, 0))
    return out


def half_of_first(bp_ref, lat_ref, half, out_ref):
    lat = lat_ref[pl.ds(pl.multiple_of(half * (H // 2), H // 2), H // 2), :]
    for z in range(4):
        part = lax.dot_general(
            bp_ref[z * 256 : (z + 1) * 256, :], lat, NT, preferred_element_type=F32
        )
        for e, piece in enumerate(arrange(part)):
            out_ref[e, z * 16 : (z + 1) * 16, :] = piece.astype(out_ref.dtype)


def back_kernel(core_ref, blk_ref, der_ref, lat_ref, w2t_ref, bp_ref, send_ref, low_ref):
    for q in range(PTS // LANES):
        parts = [blk_ref[g * GROUPS + q].astype(F32) for g in range(GROUPS)]
        parts.append(jnp.zeros((128 - PAD, LANES), F32))
        low_ref[:, q * LANES : (q + 1) * LANES] = jnp.concatenate(parts, 0).astype(BF)
    for n in range(PTS // WIDE):
        cols = slice(n * WIDE, (n + 1) * WIDE)
        back = jnp.dot(w2t_ref[...], low_ref[:, cols], preferred_element_type=F32)
        bp_ref[:, cols] = (back * der_ref[:, cols].astype(F32)).astype(BF)
    half_of_first(bp_ref, lat_ref, 1 - core_ref[0], send_ref)


def backward(core, blocks, deriv, latent, w2t):
    return pl.pallas_call(
        back_kernel,
        in_specs=[SCALAR, VM, VM, VM, VM],
        out_specs=[VM] * 3,
        out_shape=[shape((H2, PTS)), shape((16, 64, H // 2)), shape((128, PTS))],
        compiler_params=params(12),
        name="backward",
    )(core, blocks, deriv, latent, w2t)


def own_kernel(core_ref, bp_ref, lat_ref, out_ref):
    half_of_first(bp_ref, lat_ref, core_ref[0], out_ref)


def own_half(core, bp, latent):
    return pl.pallas_call(
        own_kernel,
        in_specs=[SCALAR, VM, VM],
        out_specs=VM,
        out_shape=shape((16, 64, H // 2), F32),
        compiler_params=params(12),
        cost_estimate=pl.CostEstimate(
            flops=2 * H2 * (H // 2) * PTS, bytes_accessed=8 * 1024 * 1024, transcendentals=0
        ),
        name="own_half",
    )(core, bp, latent)


def emit_kernel(low_ref, grad_ref):
    for g in range(GROUPS):
        used = min(USED, C - g * USED)
        part = low_ref[g * ROWS : (g + 1) * ROWS, :].astype(F32)
        grad_ref[g * USED : g * USED + used] = part[:used].reshape(used, 1, PTS)


def emit(low):
    return pl.pallas_call(
        emit_kernel,
        in_specs=[VM],
        out_specs=VM,
        out_shape=shape((C, 1, PTS), F32),
        compiler_params=params(6),
        cost_estimate=pl.CostEstimate(flops=0, bytes_accessed=PTS, transcendentals=0),
        name="emit",
    )(low)


def second_kernel(core_ref, low_ref, hid_ref, keep_ref, send_ref, second):
    half = H2 // 2
    second[...] = lax.dot_general(low_ref[...], hid_ref[...], NT, preferred_element_type=F32)[:PAD]
    row = lax.broadcasted_iota(jnp.int32, (8, LANES), 0)
    total = jnp.zeros((1, LANES), F32)
    for g in range(GROUPS):
        block = low_ref[g * ROWS : (g + 1) * ROWS, :].astype(F32)
        for q in range(PTS // LANES):
            cols = slice(q * LANES, (q + 1) * LANES)
            total += block[HI : HI + 1, cols] + block[LO : LO + 1, cols]
    high = total.astype(BF).astype(F32)
    top = ROWS - 8
    second[top:ROWS, :LANES] = jnp.where(
        row == HI - top,
        high,
        jnp.where(row == LO - top, total - high, second[top:ROWS, :LANES]),
    )
    keep_ref[...] = second[:, pl.ds(pl.multiple_of(core_ref[0] * half, half), half)]
    send_ref[...] = second[:, pl.ds(pl.multiple_of((1 - core_ref[0]) * half, half), half)].astype(BF)


def second_halves(core, low, hidden):
    return pl.pallas_call(
        second_kernel,
        in_specs=[SCALAR, VM, VM],
        out_specs=[VM] * 2,
        out_shape=[shape((PAD, H2 // 2), F32), shape((PAD, H2 // 2))],
        scratch_shapes=[pltpu.VMEM((PAD, H2), F32)],
        compiler_params=params(12),
        name="second",
    )(core, low, hidden)


def sum_kernel(scale, parts_ref, out_ref):
    total = parts_ref[0].astype(F32)
    for e in range(1, parts_ref.shape[0]):
        total += parts_ref[e].astype(F32)
    out_ref[...] = (total * scale).astype(out_ref.dtype)


def sum_parts(parts, scale, dtype, flops):
    return pl.pallas_call(
        functools.partial(sum_kernel, scale),
        in_specs=[VM],
        out_specs=VM,
        out_shape=shape(parts.shape[1:], dtype),
        compiler_params=params(6),
        cost_estimate=pl.CostEstimate(flops=flops, bytes_accessed=parts.size * 2, transcendentals=0),
        name="sum_parts",
    )(parts)


def halves_kernel(core_ref, parts_ref, keep_ref, give_ref):
    total = parts_ref[0].astype(F32)
    for e in range(1, parts_ref.shape[0]):
        total += parts_ref[e].astype(F32)
    total *= 1.0 / math.sqrt(MEMBERS * NPTS)
    upper, under = total[:4], total[4:]
    first_core = core_ref[0] == 0
    keep_ref[...] = jnp.where(first_core, upper, under)
    give_ref[...] = jnp.where(first_core, under, upper)


def sum_halves(core, parts):
    return pl.pallas_call(
        halves_kernel,
        in_specs=[SCALAR, VM],
        out_specs=[VM, VM],
        out_shape=[shape((4, H // 2), F32)] * 2,
        compiler_params=params(6),
        cost_estimate=pl.CostEstimate(flops=FLOPS, bytes_accessed=parts.size * 2, transcendentals=0),
        name="sum_halves",
    )(core, parts)


def finish_kernel(core_ref, keep_ref, got_ref, mine_ref, other_ref, first_ref, second_ref, loss_ref):
    half = H // 2
    first_core = core_ref[0] == 0
    keep, got = keep_ref[...], got_ref[...]
    first_ref[:, :half] = jnp.where(first_core, keep, got)
    first_ref[:, half:] = jnp.where(first_core, got, keep)
    mine, other = mine_ref[...].astype(F32), other_ref[...].astype(F32)
    left, right = jnp.where(first_core, mine, other), jnp.where(first_core, other, mine)
    loss = left[HI : HI + 1, :LANES] + left[LO : LO + 1, :LANES]
    loss_ref[...] = jnp.sum(loss, axis=1, keepdims=True) / NPTS
    scale = MEMBERS / math.sqrt(NPTS)
    for g in range(GROUPS):
        used = min(USED, C - g * USED)
        for cols, part in ((slice(0, half), left), (slice(half, H2), right)):
            rows = part[g * ROWS : g * ROWS + used] * scale
            second_ref[g * USED : g * USED + used, :, cols] = rows.reshape(used, 1, half)


def finish(core, keep, got, mine, other):
    return pl.pallas_call(
        finish_kernel,
        in_specs=[SCALAR, VM, VM, VM, VM],
        out_specs=[VM] * 3,
        out_shape=[shape((4, H), F32), shape((C, 1, H2), F32), shape((1, 1), F32)],
        compiler_params=params(6),
        name="finish",
    )(core, keep, got, mine, other)


def swap(value, axis, by):
    size = lax.axis_size(axis)
    return lax.ppermute(value, axis, [(i, i ^ by) for i in range(size)])


def cross(value, h, y):
    pairs = [(zh * 4 + k, (zh ^ h) * 4 + (k ^ y)) for zh in range(2) for k in range(4)]
    return lax.ppermute(value, ("zh", "y"), pairs)


def packed(total):
    row = lax.broadcasted_iota(jnp.int32, total.shape, 0)
    loss = total[HI : HI + 1] + total[LO : LO + 1]
    high = lax.reduce_precision(loss, 8, 7)
    return jnp.where(row == HI, high, jnp.where(row == LO, loss - high, total)).astype(BF)


def on_device(latent, truth, w_first, w_second):
    core = lax.axis_index("c").astype(jnp.int32)
    group, quarter = lax.axis_index("zl"), lax.axis_index("x")
    place = (lax.axis_index("zh") * 4 + lax.axis_index("y")) * 2 + lax.axis_index("c")
    where = jnp.stack([group, quarter, place]).astype(jnp.int32)
    latent, where, core = lax.optimization_barrier((latent, where, core[None]))

    hidden, deriv, kept_latent, blocks, w2t, truth_here, area = forward(
        where, latent, w_first, w_second, truth
    )

    gathered = lax.all_to_all(blocks, ("zl", "x"), 0, 0, tiled=True)
    grads = pairs(gathered, truth_here, area)
    grads = lax.all_to_all(grads, ("zl", "x"), 0, 0, tiled=True)

    bp, send, low = backward(core, grads, deriv, kept_latent, w2t)
    arrived = swap(send, "c", 1)
    keep2, send2 = second_halves(core, low, hidden)
    arrived2 = swap(send2, "c", 1)
    own = own_half(core, bp, kept_latent)
    first = (own + arrived.astype(F32)).astype(BF)
    total = packed(keep2 + arrived2.astype(F32))
    first, total, low = lax.optimization_barrier((first, total, low))

    field_grad = emit(low)
    near, far, both = (cross(total, h, y).astype(F32) for h, y in ((0, 1), (1, 0), (1, 1)))
    total = packed((total.astype(F32) + both) + (near + far))
    first = lax.all_to_all(first, ("x", "y"), 0, 0, tiled=True)
    first = sum_parts(first, 1.0, BF, FLOPS).reshape(8, 8, H // 2)
    first, total, field_grad = lax.optimization_barrier((first, total, field_grad))

    total = packed(total.astype(F32) + swap(total, "y", 2).astype(F32))
    first = lax.all_to_all(first, ("zl", "zh"), 0, 0, tiled=True)
    first, total = lax.optimization_barrier((first, total))

    other = swap(total, "c", 1)
    keep, give = sum_halves(core, first)
    got = swap(give, "c", 1)
    first_out, second_out, loss = finish(core, keep, got, total, other)
    return loss[0], field_grad.transpose(1, 0, 2), first_out, second_out.transpose(1, 0, 2)


def solution(mesh):
    fine = Mesh(mesh.devices.reshape(4, 4, 2, 4, 2), ("zl", "x", "zh", "y", "c"))
    ens, space = ("zl", "x"), ("zh", "y", "c")
    in_specs = (P(ens, None, space), P(None, space), P(), P())
    out_specs = (P(ens), P(ens, None, space), P(ens + space, None), P(ens, None, None))
    return jax.shard_map(
        on_device, mesh=fine, in_specs=in_specs, out_specs=out_specs, check_vma=False
    )
```

```python
import functools
import math

import jax
import jax.numpy as jnp
from jax import lax
from jax.experimental import pallas as pl
from jax.experimental.pallas import tpu as pltpu
from jax.sharding import Mesh
from jax.sharding import PartitionSpec as P

BF = jnp.bfloat16
F32 = jnp.float32
EPS = 0.01
C, H, H2 = 83, 1024, 1024
PTS = 1536
NPTS = 24576
MEMBERS = 16
GROUPS, USED, ROWS, LANES = 4, 21, 24, 384
PAD = GROUPS * ROWS
WIDE = 512
HI, LO = 21, 22
FLOPS = 20_000_000_000
NT = (((1,), (1,)), ((), ()))
VM = pl.BlockSpec(memory_space=pltpu.VMEM)
HBM = pl.BlockSpec(memory_space=pltpu.HBM)
SCALAR = pl.BlockSpec(memory_space=pltpu.SMEM)


def params(mib=24):
    return pltpu.CompilerParams(vmem_limit_bytes=mib * 1024 * 1024)


def shape(dims, dtype=BF):
    return jax.ShapeDtypeStruct(dims, dtype)


def in_hbm(value):
    return pltpu.with_memory_space_constraint(value, pltpu.HBM)


def own_tiles(where_ref, all_truth_ref, truth_ref, area_ref):
    lane_tiles = LANES // 128
    group, quarter, place = where_ref[0], where_ref[1], where_ref[2]
    cols = pl.ds(pl.multiple_of(quarter * LANES, 128), LANES)
    all_truth = jnp.concatenate(
        [all_truth_ref[:, cols].astype(F32), jnp.zeros((GROUPS * USED + ROWS - USED - C, LANES), F32)], 0
    )
    truth_here = all_truth[:ROWS]
    for g in range(1, GROUPS):
        truth_here = jnp.where(group == g, all_truth[g * USED : g * USED + ROWS], truth_here)
    lane = lax.broadcasted_iota(jnp.int32, (ROWS, LANES), 1)
    row = lax.broadcasted_iota(jnp.int32, (ROWS, LANES), 0)
    position = (place * PTS + quarter * LANES + lane).astype(F32)
    area_here = jnp.cos(math.pi * ((position + 0.5) / NPTS - 0.5))
    area_here = jnp.where((row < USED) & (group * USED + row < C), area_here, 0.0)
    for r in range(ROWS // 8):
        for l in range(lane_tiles):
            tile = (slice(r * 8, (r + 1) * 8), slice(l * 128, (l + 1) * 128))
            truth_ref[r * lane_tiles + l] = truth_here[tile]
            area_ref[r * lane_tiles + l] = area_here[tile]


def forward_kernel(
    where_ref, lat_hbm, w1_hbm, w2_hbm, truth_hbm,
    hid_ref, der_ref, lat_ref, blk_ref, w2t_ref, truth_ref, area_ref,
    w1, w2_ref, all_truth, w2p, field, sems,
):
    halves, spans = 2, PTS // WIDE
    rows = H2 // halves
    w1_in = [
        pltpu.make_async_copy(
            w1_hbm.at[r * rows : (r + 1) * rows], w1.at[r * rows : (r + 1) * rows], sems.at[r]
        )
        for r in range(halves)
    ]
    lat_in = [
        pltpu.make_async_copy(
            lat_hbm.at[0, :, n * WIDE : (n + 1) * WIDE],
            lat_ref.at[:, n * WIDE : (n + 1) * WIDE],
            sems.at[halves + n],
        )
        for n in range(spans)
    ]
    w2_in = pltpu.make_async_copy(w2_hbm, w2_ref, sems.at[halves + spans])
    truth_in = pltpu.make_async_copy(truth_hbm, all_truth, sems.at[halves + spans + 1])
    for copy in [w2_in, truth_in, w1_in[0], lat_in[0]] + w1_in[1:] + lat_in[1:]:
        copy.start()
    w2_in.wait()
    w2 = jnp.concatenate([w2_ref[...].astype(F32), jnp.zeros((1, H2), F32)], 0)
    gap = jnp.zeros((ROWS - USED, H2), F32)
    parts = []
    for g in range(GROUPS):
        parts += [w2[g * USED : (g + 1) * USED], gap]
    padded = jnp.concatenate(parts, 0)
    w2p[...] = padded.astype(BF)
    w2t_ref[...] = (0.5 * jnp.concatenate([padded, jnp.zeros((128 - PAD, H2), F32)], 0)).T.astype(BF)

    def decode(n):
        cols = slice(n * WIDE, (n + 1) * WIDE)
        field[:, cols] = jnp.dot(w2p[...], hid_ref[:, cols], preferred_element_type=F32)

    def gate(pre, here, cols):
        half = 0.5 * pre
        t = jnp.tanh(half)
        twice = 1.0 + t
        act = half * twice
        hid_ref[here, cols] = act.astype(BF)
        der_ref[here, cols] = (twice + act * (1.0 - t)).astype(BF)

    held = None
    for n in range(spans):
        if n == 0:
            lat_in[0].wait()
        if n == 1:
            truth_in.wait()
            for copy in lat_in[1:]:
                copy.wait()
            own_tiles(where_ref, all_truth, truth_ref, area_ref)
        cols = slice(n * WIDE, (n + 1) * WIDE)
        for r in range(0, H2, 128):
            if n == 0 and r % rows == 0:
                w1_in[r // rows].wait()
            here = slice(r, r + 128)
            pre = jnp.dot(w1[here, :], lat_ref[:, cols], preferred_element_type=F32)
            if held is not None:
                gate(*held)
            held = (pre, here, cols)
        if n > 0:
            decode(n - 1)
    gate(*held)
    decode(spans - 1)
    for g in range(GROUPS):
        for q in range(PTS // LANES):
            blk_ref[q * GROUPS + g] = field[
                g * ROWS : (g + 1) * ROWS, q * LANES : (q + 1) * LANES
            ].astype(BF)


def forward(where, latent, w_first, w_second, truth):
    spots = ROWS // 8 * (LANES // 128)
    return pl.pallas_call(
        forward_kernel,
        in_specs=[SCALAR, HBM, HBM, HBM, HBM],
        out_specs=[VM] * 7,
        out_shape=[
            shape((H2, PTS)),
            shape((H2, PTS)),
            shape((H, PTS)),
            shape((16, ROWS, LANES)),
            shape((H2, 128)),
            shape((spots, 8, 128), F32),
            shape((spots, 8, 128), F32),
        ],
        scratch_shapes=[
            pltpu.VMEM((H2, H), BF),
            pltpu.VMEM((C, H2), BF),
            pltpu.VMEM((C, PTS), BF),
            pltpu.VMEM((PAD, H2), BF),
            pltpu.VMEM((PAD, PTS), F32),
            pltpu.SemaphoreType.DMA((4 + PTS // WIDE,)),
        ],
        compiler_params=params(12),
        name="forward",
    )(where, in_hbm(latent), in_hbm(w_first), in_hbm(w_second), in_hbm(truth))


def pair_kernel(fields_ref, truth_ref, area_ref, out_ref, values, grads):
    lane_tiles = LANES // 128
    for m in range(MEMBERS):
        block = fields_ref[m].astype(F32)
        for r in range(ROWS // 8):
            for l in range(lane_tiles):
                values[r * lane_tiles + l, m] = block[
                    r * 8 : (r + 1) * 8, l * 128 : (l + 1) * 128
                ]

    def spot(index, losses):
        v = [values[index, m] for m in range(MEMBERS)]
        truth = truth_ref[index]
        area = area_ref[index]
        value = [None] * MEMBERS
        slope = [None] * MEMBERS

        def add(store, m, term):
            store[m] = term if store[m] is None else store[m] + term

        for m in range(MEMBERS):
            for k in range(m + 1, MEMBERS):
                d = v[m] - v[k]
                square = d * d + EPS
                inverse = lax.rsqrt(square)
                s = square * inverse
                t = d * inverse
                add(value, m, s)
                add(value, k, s)
                add(slope, m, t)
                slope[k] = -t if slope[k] is None else slope[k] - t
        new = []
        for m in range(MEMBERS):
            gap = v[m] - truth
            square = gap * gap + EPS
            inverse = lax.rsqrt(square)
            grads[index, m] = area * (
                gap * inverse * (1.0 / MEMBERS)
                - slope[m] * (1.0 / (MEMBERS * (MEMBERS - 1)))
            )
            new.append(area * (square * inverse - value[m] * (1.0 / (2.0 * (MEMBERS - 1)))))
        return [a + b for a, b in zip(losses, new)]

    zero = [jnp.zeros((8, 128), F32) for _ in range(MEMBERS)]
    row = lax.broadcasted_iota(jnp.int32, (8, 128), 0)
    last = ROWS // 8 - 1
    for l in range(lane_tiles):
        losses = lax.fori_loop(
            0, ROWS // 8, lambda r, carry: spot(r * lane_tiles + l, carry), zero
        )
        for m in range(MEMBERS):
            loss = jnp.sum(losses[m], axis=0, keepdims=True)
            high = loss.astype(BF).astype(F32)
            low = loss - high
            at = last * lane_tiles + l
            kept = grads[at, m]
            grads[at, m] = jnp.where(
                row == HI - 8 * last, high, jnp.where(row == LO - 8 * last, low, kept)
            )
    for m in range(MEMBERS):
        out_ref[m] = jnp.concatenate(
            [
                jnp.concatenate([grads[r * lane_tiles + l, m] for l in range(lane_tiles)], 1)
                for r in range(ROWS // 8)
            ],
            0,
        ).astype(BF)


def pairs(fields, truth, area):
    spots = ROWS // 8 * (LANES // 128)
    return pl.pallas_call(
        pair_kernel,
        out_shape=shape((16, ROWS, LANES)),
        in_specs=[VM] * 3,
        out_specs=VM,
        scratch_shapes=[
            pltpu.VMEM((spots, MEMBERS, 8, 128), F32),
            pltpu.VMEM((spots, MEMBERS, 8, 128), F32),
        ],
        compiler_params=params(6),
        name="pairs",
    )(fields, truth, area)


def arrange(rows):
    out = []
    for y in range(4):
        for x in range(4):
            pick = [rows[x * 64 + zh * 32 + y * 8 : x * 64 + zh * 32 + y * 8 + 8] for zh in range(2)]
            out.append(jnp.concatenate(pick, 0))
    return out


def half_of_first(bp_ref, lat_ref, half, out_ref):
    lat = lat_ref[pl.ds(pl.multiple_of(half * (H // 2), H // 2), H // 2), :]
    for z in range(4):
        part = lax.dot_general(
            bp_ref[z * 256 : (z + 1) * 256, :], lat, NT, preferred_element_type=F32
        )
        for e, piece in enumerate(arrange(part)):
            out_ref[e, z * 16 : (z + 1) * 16, :] = piece.astype(out_ref.dtype)


def back_kernel(core_ref, blk_ref, der_ref, lat_ref, w2t_ref, bp_ref, send_ref, low_ref):
    for q in range(PTS // LANES):
        parts = [blk_ref[q * GROUPS + g].astype(F32) for g in range(GROUPS)]
        parts.append(jnp.zeros((128 - PAD, LANES), F32))
        low_ref[:, q * LANES : (q + 1) * LANES] = jnp.concatenate(parts, 0).astype(BF)
    for n in range(PTS // WIDE):
        cols = slice(n * WIDE, (n + 1) * WIDE)
        back = jnp.dot(w2t_ref[...], low_ref[:, cols], preferred_element_type=F32)
        bp_ref[:, cols] = (back * der_ref[:, cols].astype(F32)).astype(BF)
    half_of_first(bp_ref, lat_ref, 1 - core_ref[0], send_ref)


def backward(core, blocks, deriv, latent, w2t):
    return pl.pallas_call(
        back_kernel,
        in_specs=[SCALAR, VM, VM, VM, VM],
        out_specs=[VM] * 3,
        out_shape=[shape((H2, PTS)), shape((16, 64, H // 2)), shape((128, PTS))],
        compiler_params=params(12),
        name="backward",
    )(core, blocks, deriv, latent, w2t)


def own_kernel(core_ref, bp_ref, lat_ref, out_ref):
    half_of_first(bp_ref, lat_ref, core_ref[0], out_ref)


def own_half(core, bp, latent):
    return pl.pallas_call(
        own_kernel,
        in_specs=[SCALAR, VM, VM],
        out_specs=VM,
        out_shape=shape((16, 64, H // 2), F32),
        compiler_params=params(12),
        cost_estimate=pl.CostEstimate(
            flops=2 * H2 * (H // 2) * PTS, bytes_accessed=8 * 1024 * 1024, transcendentals=0
        ),
        name="own_half",
    )(core, bp, latent)


def emit_kernel(low_ref, grad_ref):
    for g in range(GROUPS):
        used = min(USED, C - g * USED)
        part = low_ref[g * ROWS : (g + 1) * ROWS, :].astype(F32)
        grad_ref[g * USED : g * USED + used] = part[:used].reshape(used, 1, PTS)


def emit(low):
    return pl.pallas_call(
        emit_kernel,
        in_specs=[VM],
        out_specs=VM,
        out_shape=shape((C, 1, PTS), F32),
        compiler_params=params(6),
        cost_estimate=pl.CostEstimate(flops=0, bytes_accessed=PTS, transcendentals=0),
        name="emit",
    )(low)


def second_kernel(core_ref, low_ref, hid_ref, keep_ref, send_ref, second):
    half = H2 // 2
    second[...] = lax.dot_general(low_ref[...], hid_ref[...], NT, preferred_element_type=F32)[:PAD]
    row = lax.broadcasted_iota(jnp.int32, (8, LANES), 0)
    total = jnp.zeros((1, LANES), F32)
    for g in range(GROUPS):
        block = low_ref[g * ROWS : (g + 1) * ROWS, :].astype(F32)
        for q in range(PTS // LANES):
            cols = slice(q * LANES, (q + 1) * LANES)
            total += block[HI : HI + 1, cols] + block[LO : LO + 1, cols]
    high = total.astype(BF).astype(F32)
    top = ROWS - 8
    second[top:ROWS, :LANES] = jnp.where(
        row == HI - top,
        high,
        jnp.where(row == LO - top, total - high, second[top:ROWS, :LANES]),
    )
    keep_ref[...] = second[:, pl.ds(pl.multiple_of(core_ref[0] * half, half), half)]
    send_ref[...] = second[:, pl.ds(pl.multiple_of((1 - core_ref[0]) * half, half), half)].astype(BF)


def second_halves(core, low, hidden):
    return pl.pallas_call(
        second_kernel,
        in_specs=[SCALAR, VM, VM],
        out_specs=[VM] * 2,
        out_shape=[shape((PAD, H2 // 2), F32), shape((PAD, H2 // 2))],
        scratch_shapes=[pltpu.VMEM((PAD, H2), F32)],
        compiler_params=params(12),
        name="second",
    )(core, low, hidden)


def total_of(parts_ref, which):
    total = parts_ref[which[0]].astype(F32)
    for e in which[1:]:
        total += parts_ref[e].astype(F32)
    return total


def sum_chips_kernel(parts_ref, out_ref):
    total = total_of(parts_ref, range(16))
    for z in range(8):
        for c in range(2):
            at = z * 8 + c * 4
            out_ref[c * 8 + z] = total[at : at + 4].astype(BF)


def sum_chips(parts):
    return pl.pallas_call(
        sum_chips_kernel,
        in_specs=[VM],
        out_specs=VM,
        out_shape=shape((16, 4, H // 2)),
        compiler_params=params(6),
        cost_estimate=pl.CostEstimate(flops=FLOPS, bytes_accessed=parts.size * 2, transcendentals=0),
        name="sum_chips",
    )(parts)


def sum_last_kernel(parts_ref, out_ref):
    half = H // 2
    for c in range(2):
        total = total_of(parts_ref, range(c * 8, c * 8 + 8))
        out_ref[:, c * half : (c + 1) * half] = total * (1.0 / math.sqrt(MEMBERS * NPTS))


def sum_last(parts):
    return pl.pallas_call(
        sum_last_kernel,
        in_specs=[VM],
        out_specs=VM,
        out_shape=shape((4, H), F32),
        compiler_params=params(6),
        cost_estimate=pl.CostEstimate(flops=FLOPS, bytes_accessed=parts.size * 2, transcendentals=0),
        name="sum_last",
    )(parts)


def finish_kernel(core_ref, mine_ref, other_ref, second_ref, loss_ref):
    half = H // 2
    first_core = core_ref[0] == 0
    mine, other = mine_ref[...].astype(F32), other_ref[...].astype(F32)
    left, right = jnp.where(first_core, mine, other), jnp.where(first_core, other, mine)
    loss = left[HI : HI + 1, :LANES] + left[LO : LO + 1, :LANES]
    loss_ref[...] = jnp.sum(loss, axis=1, keepdims=True) / NPTS
    scale = MEMBERS / math.sqrt(NPTS)
    for g in range(GROUPS):
        used = min(USED, C - g * USED)
        for cols, part in ((slice(0, half), left), (slice(half, H2), right)):
            rows = part[g * ROWS : g * ROWS + used] * scale
            second_ref[g * USED : g * USED + used, :, cols] = rows.reshape(used, 1, half)


def finish(core, mine, other):
    return pl.pallas_call(
        finish_kernel,
        in_specs=[SCALAR, VM, VM],
        out_specs=[VM] * 2,
        out_shape=[shape((C, 1, H2), F32), shape((1, 1), F32)],
        compiler_params=params(6),
        cost_estimate=pl.CostEstimate(flops=0, bytes_accessed=PTS, transcendentals=0),
        name="finish",
    )(core, mine, other)


def swap(value, axis, by):
    size = lax.axis_size(axis)
    return lax.ppermute(value, axis, [(i, i ^ by) for i in range(size)])


def cross(value, h, y):
    pairs = [(zh * 4 + k, (zh ^ h) * 4 + (k ^ y)) for zh in range(2) for k in range(4)]
    return lax.ppermute(value, ("zh", "y"), pairs)


def packed(total):
    row = lax.broadcasted_iota(jnp.int32, total.shape, 0)
    loss = total[HI : HI + 1] + total[LO : LO + 1]
    high = lax.reduce_precision(loss, 8, 7)
    return jnp.where(row == HI, high, jnp.where(row == LO, loss - high, total)).astype(BF)


def on_device(latent, truth, w_first, w_second):
    core = lax.axis_index("c").astype(jnp.int32)
    group, quarter = lax.axis_index("zl"), lax.axis_index("x")
    place = (lax.axis_index("zh") * 4 + lax.axis_index("y")) * 2 + lax.axis_index("c")
    where = jnp.stack([group, quarter, place]).astype(jnp.int32)
    latent, where, core = lax.optimization_barrier((latent, where, core[None]))

    hidden, deriv, kept_latent, blocks, w2t, truth_here, area = forward(
        where, latent, w_first, w_second, truth
    )

    gathered = lax.all_to_all(blocks, ("x", "zl"), 0, 0, tiled=True)
    grads = pairs(gathered, truth_here, area)
    grads = lax.all_to_all(grads, ("x", "zl"), 0, 0, tiled=True)

    bp, send, low = backward(core, grads, deriv, kept_latent, w2t)
    arrived = swap(send, "c", 1)
    keep2, send2 = second_halves(core, low, hidden)
    arrived2 = swap(send2, "c", 1)
    own = own_half(core, bp, kept_latent)
    first = (own + arrived.astype(F32)).astype(BF)
    total = packed(keep2 + arrived2.astype(F32))
    first, total, low = lax.optimization_barrier((first, total, low))

    field_grad = emit(low)
    near, far, both = (cross(total, h, y).astype(F32) for h, y in ((0, 1), (1, 0), (1, 1)))
    total = packed((total.astype(F32) + both) + (near + far))
    first = lax.all_to_all(first, ("y", "x"), 0, 0, tiled=True)
    first = sum_chips(first)
    first, total, field_grad = lax.optimization_barrier((first, total, field_grad))

    total = packed(total.astype(F32) + swap(total, "y", 2).astype(F32))
    second_out, loss = finish(core, total, swap(total, "c", 1))
    first = lax.all_to_all(first, ("c", "zl", "zh"), 0, 0, tiled=True)
    first, second_out, loss = lax.optimization_barrier((first, second_out, loss))
    return loss[0], field_grad.transpose(1, 0, 2), sum_last(first), second_out.transpose(1, 0, 2)


def solution(mesh):
    fine = Mesh(mesh.devices.reshape(4, 4, 2, 4, 2), ("zl", "x", "zh", "y", "c"))
    ens, space = ("zl", "x"), ("zh", "y", "c")
    in_specs = (P(ens, None, space), P(None, space), P(), P())
    out_specs = (P(ens), P(ens, None, space), P(ens + space, None), P(ens, None, None))
    return jax.shard_map(
        on_device, mesh=fine, in_specs=in_specs, out_specs=out_specs, check_vma=False
    )
```

```python
import functools
import math

import jax
import jax.numpy as jnp
from jax import lax
from jax.experimental import pallas as pl
from jax.experimental.pallas import tpu as pltpu
from jax.sharding import Mesh
from jax.sharding import PartitionSpec as P

BF = jnp.bfloat16
F32 = jnp.float32
EPS = 0.01
C, H, H2 = 83, 1024, 1024
PTS = 1536
NPTS = 24576
MEMBERS = 16
GROUPS, USED, ROWS, LANES = 4, 21, 24, 384
PAD = GROUPS * ROWS
WIDE = 512
HI, LO = 21, 22
FLOPS = 20_000_000_000
NT = (((1,), (1,)), ((), ()))
VM = pl.BlockSpec(memory_space=pltpu.VMEM)
HBM = pl.BlockSpec(memory_space=pltpu.HBM)
SCALAR = pl.BlockSpec(memory_space=pltpu.SMEM)


def params(mib=24):
    return pltpu.CompilerParams(vmem_limit_bytes=mib * 1024 * 1024)


def shape(dims, dtype=BF):
    return jax.ShapeDtypeStruct(dims, dtype)


def in_hbm(value):
    return pltpu.with_memory_space_constraint(value, pltpu.HBM)


def own_tiles(where_ref, all_truth_ref, truth_ref, area_ref):
    lane_tiles = LANES // 128
    group, quarter, place = where_ref[0], where_ref[1], where_ref[2]
    cols = pl.ds(pl.multiple_of(quarter * LANES, 128), LANES)
    all_truth = jnp.concatenate(
        [all_truth_ref[:, cols].astype(F32), jnp.zeros((GROUPS * USED + ROWS - USED - C, LANES), F32)], 0
    )
    truth_here = all_truth[:ROWS]
    for g in range(1, GROUPS):
        truth_here = jnp.where(group == g, all_truth[g * USED : g * USED + ROWS], truth_here)
    lane = lax.broadcasted_iota(jnp.int32, (ROWS, LANES), 1)
    row = lax.broadcasted_iota(jnp.int32, (ROWS, LANES), 0)
    position = (place * PTS + quarter * LANES + lane).astype(F32)
    area_here = jnp.cos(math.pi * ((position + 0.5) / NPTS - 0.5))
    area_here = jnp.where((row < USED) & (group * USED + row < C), area_here, 0.0)
    for r in range(ROWS // 8):
        for l in range(lane_tiles):
            tile = (slice(r * 8, (r + 1) * 8), slice(l * 128, (l + 1) * 128))
            truth_ref[r * lane_tiles + l] = truth_here[tile]
            area_ref[r * lane_tiles + l] = area_here[tile]


def forward_kernel(
    where_ref, lat_hbm, w1_hbm, w2_hbm, truth_hbm,
    hid_ref, der_ref, lat_ref, blk_ref, w2t_ref, truth_ref, area_ref,
    w1, w2_ref, all_truth, w2p, field, sems,
):
    halves, spans = 2, PTS // WIDE
    rows = H2 // halves
    w1_in = [
        pltpu.make_async_copy(
            w1_hbm.at[r * rows : (r + 1) * rows], w1.at[r * rows : (r + 1) * rows], sems.at[r]
        )
        for r in range(halves)
    ]
    lat_in = [
        pltpu.make_async_copy(
            lat_hbm.at[0, :, n * WIDE : (n + 1) * WIDE],
            lat_ref.at[:, n * WIDE : (n + 1) * WIDE],
            sems.at[halves + n],
        )
        for n in range(spans)
    ]
    w2_in = pltpu.make_async_copy(w2_hbm, w2_ref, sems.at[halves + spans])
    truth_in = pltpu.make_async_copy(truth_hbm, all_truth, sems.at[halves + spans + 1])
    for copy in [w2_in, truth_in, w1_in[0], lat_in[0]] + w1_in[1:] + lat_in[1:]:
        copy.start()
    w2_in.wait()
    w2 = jnp.concatenate([w2_ref[...].astype(F32), jnp.zeros((1, H2), F32)], 0)
    gap = jnp.zeros((ROWS - USED, H2), F32)
    parts = []
    for g in range(GROUPS):
        parts += [w2[g * USED : (g + 1) * USED], gap]
    padded = jnp.concatenate(parts, 0)
    w2p[...] = padded.astype(BF)
    w2t_ref[...] = (0.5 * jnp.concatenate([padded, jnp.zeros((128 - PAD, H2), F32)], 0)).T.astype(BF)

    def decode(n):
        cols = slice(n * WIDE, (n + 1) * WIDE)
        field[:, cols] = jnp.dot(w2p[...], hid_ref[:, cols], preferred_element_type=F32)

    def gate(pre, here, cols):
        half = 0.5 * pre
        t = jnp.tanh(half)
        twice = 1.0 + t
        act = half * twice
        hid_ref[here, cols] = act.astype(BF)
        der_ref[here, cols] = (twice + act * (1.0 - t)).astype(BF)

    held = None
    for n in range(spans):
        if n == 0:
            lat_in[0].wait()
        if n == 1:
            truth_in.wait()
            for copy in lat_in[1:]:
                copy.wait()
            own_tiles(where_ref, all_truth, truth_ref, area_ref)
        cols = slice(n * WIDE, (n + 1) * WIDE)
        for r in range(0, H2, 128):
            if n == 0 and r % rows == 0:
                w1_in[r // rows].wait()
            here = slice(r, r + 128)
            pre = jnp.dot(w1[here, :], lat_ref[:, cols], preferred_element_type=F32)
            if held is not None:
                gate(*held)
            held = (pre, here, cols)
        if n > 0:
            decode(n - 1)
    gate(*held)
    decode(spans - 1)
    for g in range(GROUPS):
        for q in range(PTS // LANES):
            blk_ref[q * GROUPS + g] = field[
                g * ROWS : (g + 1) * ROWS, q * LANES : (q + 1) * LANES
            ].astype(BF)


def forward(where, latent, w_first, w_second, truth):
    spots = ROWS // 8 * (LANES // 128)
    return pl.pallas_call(
        forward_kernel,
        in_specs=[SCALAR, HBM, HBM, HBM, HBM],
        out_specs=[VM] * 7,
        out_shape=[
            shape((H2, PTS)),
            shape((H2, PTS)),
            shape((H, PTS)),
            shape((16, ROWS, LANES)),
            shape((H2, 128)),
            shape((spots, 8, 128), F32),
            shape((spots, 8, 128), F32),
        ],
        scratch_shapes=[
            pltpu.VMEM((H2, H), BF),
            pltpu.VMEM((C, H2), BF),
            pltpu.VMEM((C, PTS), BF),
            pltpu.VMEM((PAD, H2), BF),
            pltpu.VMEM((PAD, PTS), F32),
            pltpu.SemaphoreType.DMA((4 + PTS // WIDE,)),
        ],
        compiler_params=params(12),
        name="forward",
    )(where, in_hbm(latent), in_hbm(w_first), in_hbm(w_second), in_hbm(truth))


def pair_kernel(fields_ref, truth_ref, area_ref, out_ref, values, grads):
    lane_tiles = LANES // 128
    for m in range(MEMBERS):
        block = fields_ref[m].astype(F32)
        for r in range(ROWS // 8):
            for l in range(lane_tiles):
                values[r * lane_tiles + l, m] = block[
                    r * 8 : (r + 1) * 8, l * 128 : (l + 1) * 128
                ]

    def spot(index, losses):
        v = [values[index, m] for m in range(MEMBERS)]
        truth = truth_ref[index]
        area = area_ref[index]
        value = [None] * MEMBERS
        slope = [None] * MEMBERS

        def add(store, m, term):
            store[m] = term if store[m] is None else store[m] + term

        for m in range(MEMBERS):
            for k in range(m + 1, MEMBERS):
                d = v[m] - v[k]
                square = d * d + EPS
                inverse = lax.rsqrt(square)
                s = square * inverse
                t = d * inverse
                add(value, m, s)
                add(value, k, s)
                add(slope, m, t)
                slope[k] = -t if slope[k] is None else slope[k] - t
        new = []
        for m in range(MEMBERS):
            gap = v[m] - truth
            square = gap * gap + EPS
            inverse = lax.rsqrt(square)
            grads[index, m] = area * (
                gap * inverse * (1.0 / MEMBERS)
                - slope[m] * (1.0 / (MEMBERS * (MEMBERS - 1)))
            )
            new.append(area * (square * inverse - value[m] * (1.0 / (2.0 * (MEMBERS - 1)))))
        return [a + b for a, b in zip(losses, new)]

    zero = [jnp.zeros((8, 128), F32) for _ in range(MEMBERS)]
    row = lax.broadcasted_iota(jnp.int32, (8, 128), 0)
    last = ROWS // 8 - 1
    for l in range(lane_tiles):
        losses = lax.fori_loop(
            0, ROWS // 8, lambda r, carry: spot(r * lane_tiles + l, carry), zero
        )
        for m in range(MEMBERS):
            loss = jnp.sum(losses[m], axis=0, keepdims=True)
            high = loss.astype(BF).astype(F32)
            low = loss - high
            at = last * lane_tiles + l
            kept = grads[at, m]
            grads[at, m] = jnp.where(
                row == HI - 8 * last, high, jnp.where(row == LO - 8 * last, low, kept)
            )
    for m in range(MEMBERS):
        out_ref[m] = jnp.concatenate(
            [
                jnp.concatenate([grads[r * lane_tiles + l, m] for l in range(lane_tiles)], 1)
                for r in range(ROWS // 8)
            ],
            0,
        ).astype(BF)


def pairs(fields, truth, area):
    spots = ROWS // 8 * (LANES // 128)
    return pl.pallas_call(
        pair_kernel,
        out_shape=shape((16, ROWS, LANES)),
        in_specs=[VM] * 3,
        out_specs=VM,
        scratch_shapes=[
            pltpu.VMEM((spots, MEMBERS, 8, 128), F32),
            pltpu.VMEM((spots, MEMBERS, 8, 128), F32),
        ],
        compiler_params=params(6),
        name="pairs",
    )(fields, truth, area)


def arrange(rows):
    out = []
    for y in range(4):
        for x in range(4):
            pick = [rows[x * 64 + zh * 32 + y * 8 : x * 64 + zh * 32 + y * 8 + 8] for zh in range(2)]
            out.append(jnp.concatenate(pick, 0))
    return out


def half_of_first(bp_ref, lat_ref, half, out_ref):
    lat = lat_ref[pl.ds(pl.multiple_of(half * (H // 2), H // 2), H // 2), :]
    for z in range(4):
        part = lax.dot_general(
            bp_ref[z * 256 : (z + 1) * 256, :], lat, NT, preferred_element_type=F32
        )
        for e, piece in enumerate(arrange(part)):
            out_ref[e, z * 16 : (z + 1) * 16, :] = piece.astype(out_ref.dtype)


def back_kernel(core_ref, blk_ref, der_ref, lat_ref, w2t_ref, bp_ref, send_ref, low_ref):
    for q in range(PTS // LANES):
        parts = [blk_ref[q * GROUPS + g].astype(F32) for g in range(GROUPS)]
        parts.append(jnp.zeros((128 - PAD, LANES), F32))
        low_ref[:, q * LANES : (q + 1) * LANES] = jnp.concatenate(parts, 0).astype(BF)
    for n in range(PTS // WIDE):
        cols = slice(n * WIDE, (n + 1) * WIDE)
        back = jnp.dot(w2t_ref[...], low_ref[:, cols], preferred_element_type=F32)
        bp_ref[:, cols] = (back * der_ref[:, cols].astype(F32)).astype(BF)
    half_of_first(bp_ref, lat_ref, 1 - core_ref[0], send_ref)


def backward(core, blocks, deriv, latent, w2t):
    return pl.pallas_call(
        back_kernel,
        in_specs=[SCALAR, VM, VM, VM, VM],
        out_specs=[VM] * 3,
        out_shape=[shape((H2, PTS)), shape((16, 64, H // 2)), shape((128, PTS))],
        compiler_params=params(12),
        name="backward",
    )(core, blocks, deriv, latent, w2t)


def own_kernel(core_ref, bp_ref, lat_ref, out_ref):
    half_of_first(bp_ref, lat_ref, core_ref[0], out_ref)


def own_half(core, bp, latent):
    return pl.pallas_call(
        own_kernel,
        in_specs=[SCALAR, VM, VM],
        out_specs=VM,
        out_shape=shape((16, 64, H // 2), F32),
        compiler_params=params(12),
        cost_estimate=pl.CostEstimate(
            flops=2 * H2 * (H // 2) * PTS, bytes_accessed=8 * 1024 * 1024, transcendentals=0
        ),
        name="own_half",
    )(core, bp, latent)


def emit_kernel(low_ref, grad_ref):
    for g in range(GROUPS):
        used = min(USED, C - g * USED)
        part = low_ref[g * ROWS : (g + 1) * ROWS, :].astype(F32)
        grad_ref[g * USED : g * USED + used] = part[:used].reshape(used, 1, PTS)


def emit(low):
    return pl.pallas_call(
        emit_kernel,
        in_specs=[VM],
        out_specs=VM,
        out_shape=shape((C, 1, PTS), F32),
        compiler_params=params(6),
        cost_estimate=pl.CostEstimate(flops=0, bytes_accessed=PTS, transcendentals=0),
        name="emit",
    )(low)


def second_kernel(core_ref, low_ref, hid_ref, keep_ref, send_ref, second):
    half = H2 // 2
    second[...] = lax.dot_general(low_ref[...], hid_ref[...], NT, preferred_element_type=F32)[:PAD]
    row = lax.broadcasted_iota(jnp.int32, (8, LANES), 0)
    total = jnp.zeros((1, LANES), F32)
    for g in range(GROUPS):
        block = low_ref[g * ROWS : (g + 1) * ROWS, :].astype(F32)
        for q in range(PTS // LANES):
            cols = slice(q * LANES, (q + 1) * LANES)
            total += block[HI : HI + 1, cols] + block[LO : LO + 1, cols]
    high = total.astype(BF).astype(F32)
    top = ROWS - 8
    second[top:ROWS, :LANES] = jnp.where(
        row == HI - top,
        high,
        jnp.where(row == LO - top, total - high, second[top:ROWS, :LANES]),
    )
    keep_ref[...] = second[:, pl.ds(pl.multiple_of(core_ref[0] * half, half), half)]
    send_ref[...] = second[:, pl.ds(pl.multiple_of((1 - core_ref[0]) * half, half), half)].astype(BF)


def second_halves(core, low, hidden):
    return pl.pallas_call(
        second_kernel,
        in_specs=[SCALAR, VM, VM],
        out_specs=[VM] * 2,
        out_shape=[shape((PAD, H2 // 2), F32), shape((PAD, H2 // 2))],
        scratch_shapes=[pltpu.VMEM((PAD, H2), F32)],
        compiler_params=params(12),
        name="second",
    )(core, low, hidden)


def total_of(parts_ref, which):
    total = parts_ref[which[0]].astype(F32)
    for e in which[1:]:
        total += parts_ref[e].astype(F32)
    return total


def sum_chips_kernel(parts_ref, out_ref):
    total = total_of(parts_ref, range(16))
    for z in range(8):
        for c in range(2):
            at = z * 8 + c * 4
            out_ref[c * 8 + z] = total[at : at + 4].astype(BF)


def sum_chips(parts):
    return pl.pallas_call(
        sum_chips_kernel,
        in_specs=[VM],
        out_specs=VM,
        out_shape=shape((16, 4, H // 2)),
        compiler_params=params(6),
        cost_estimate=pl.CostEstimate(flops=FLOPS, bytes_accessed=parts.size * 2, transcendentals=0),
        name="sum_chips",
    )(parts)


def sum_last_kernel(parts_ref, out_ref):
    half = H // 2
    for c in range(2):
        total = total_of(parts_ref, range(c * 8, c * 8 + 8))
        out_ref[:, c * half : (c + 1) * half] = total * (1.0 / math.sqrt(MEMBERS * NPTS))


def sum_last(parts):
    return pl.pallas_call(
        sum_last_kernel,
        in_specs=[VM],
        out_specs=VM,
        out_shape=shape((4, H), F32),
        compiler_params=params(6),
        cost_estimate=pl.CostEstimate(flops=FLOPS, bytes_accessed=parts.size * 2, transcendentals=0),
        name="sum_last",
    )(parts)


def finish_kernel(core_ref, mine_ref, other_ref, second_ref, loss_ref):
    half = H // 2
    first_core = core_ref[0] == 0
    mine, other = mine_ref[...].astype(F32), other_ref[...].astype(F32)
    left, right = jnp.where(first_core, mine, other), jnp.where(first_core, other, mine)
    loss = left[HI : HI + 1, :LANES] + left[LO : LO + 1, :LANES]
    loss_ref[...] = jnp.sum(loss, axis=1, keepdims=True) / NPTS
    scale = MEMBERS / math.sqrt(NPTS)
    for g in range(GROUPS):
        used = min(USED, C - g * USED)
        for cols, part in ((slice(0, half), left), (slice(half, H2), right)):
            rows = part[g * ROWS : g * ROWS + used] * scale
            second_ref[g * USED : g * USED + used, :, cols] = rows.reshape(used, 1, half)


def finish(core, mine, other):
    return pl.pallas_call(
        finish_kernel,
        in_specs=[SCALAR, VM, VM],
        out_specs=[VM] * 2,
        out_shape=[shape((C, 1, H2), F32), shape((1, 1), F32)],
        compiler_params=params(6),
        cost_estimate=pl.CostEstimate(flops=0, bytes_accessed=PTS, transcendentals=0),
        name="finish",
    )(core, mine, other)


def swap(value, axis, by):
    size = lax.axis_size(axis)
    return lax.ppermute(value, axis, [(i, i ^ by) for i in range(size)])


def cross(value, h, y):
    pairs = []
    for zh in range(2):
        for k in range(4):
            for c in range(2):
                mate = (k + (1 if k % 2 == c else 3)) % 4 if y else k
                pairs.append(((zh * 4 + k) * 2 + c, ((zh ^ h) * 4 + mate) * 2 + c))
    return lax.ppermute(value, ("zh", "y", "c"), pairs)


def packed(total):
    row = lax.broadcasted_iota(jnp.int32, total.shape, 0)
    loss = total[HI : HI + 1] + total[LO : LO + 1]
    high = lax.reduce_precision(loss, 8, 7)
    return jnp.where(row == HI, high, jnp.where(row == LO, loss - high, total)).astype(BF)


def on_device(latent, truth, w_first, w_second):
    core = lax.axis_index("c").astype(jnp.int32)
    group, quarter = lax.axis_index("zl"), lax.axis_index("x")
    place = (lax.axis_index("zh") * 4 + lax.axis_index("y")) * 2 + lax.axis_index("c")
    where = jnp.stack([group, quarter, place]).astype(jnp.int32)
    latent, where, core = lax.optimization_barrier((latent, where, core[None]))

    hidden, deriv, kept_latent, blocks, w2t, truth_here, area = forward(
        where, latent, w_first, w_second, truth
    )

    gathered = lax.all_to_all(blocks, ("x", "zl"), 0, 0, tiled=True)
    grads = pairs(gathered, truth_here, area)
    grads = lax.all_to_all(grads, ("x", "zl"), 0, 0, tiled=True)

    bp, send, low = backward(core, grads, deriv, kept_latent, w2t)
    arrived = swap(send, "c", 1)
    keep2, send2 = second_halves(core, low, hidden)
    arrived2 = swap(send2, "c", 1)
    own = own_half(core, bp, kept_latent)
    first = (own + arrived.astype(F32)).astype(BF)
    total = packed(keep2 + arrived2.astype(F32))
    first, total, low = lax.optimization_barrier((first, total, low))

    field_grad = emit(low)
    near, far, both = (cross(total, h, y).astype(F32) for h, y in ((0, 1), (1, 0), (1, 1)))
    total = packed((total.astype(F32) + both) + (near + far))
    first = lax.all_to_all(first, ("y", "x"), 0, 0, tiled=True)
    first = sum_chips(first)
    first, total, field_grad = lax.optimization_barrier((first, total, field_grad))

    total = packed(total.astype(F32) + swap(total, "y", 2).astype(F32))
    second_out, loss = finish(core, total, swap(total, "c", 1))
    first = lax.all_to_all(first, ("c", "zl", "zh"), 0, 0, tiled=True)
    first, second_out, loss = lax.optimization_barrier((first, second_out, loss))
    return loss[0], field_grad.transpose(1, 0, 2), sum_last(first), second_out.transpose(1, 0, 2)


def solution(mesh):
    fine = Mesh(mesh.devices.reshape(4, 4, 2, 4, 2), ("zl", "x", "zh", "y", "c"))
    ens, space = ("zl", "x"), ("zh", "y", "c")
    in_specs = (P(ens, None, space), P(None, space), P(), P())
    out_specs = (P(ens), P(ens, None, space), P(ens + space, None), P(ens, None, None))
    return jax.shard_map(
        on_device, mesh=fine, in_specs=in_specs, out_specs=out_specs, check_vma=False
    )
```

```python
import functools
import math

import jax
import jax.numpy as jnp
from jax import lax
from jax.experimental import pallas as pl
from jax.experimental.pallas import tpu as pltpu
from jax.sharding import Mesh
from jax.sharding import PartitionSpec as P

BF = jnp.bfloat16
F32 = jnp.float32
EPS = 0.01
C, H, H2 = 83, 1024, 1024
PTS = 1536
NPTS = 24576
MEMBERS = 16
GROUPS, USED, ROWS, LANES = 4, 21, 24, 384
PAD = GROUPS * ROWS
WIDE = 512
HI, LO = 21, 22
FLOPS = 20_000_000_000
NT = (((1,), (1,)), ((), ()))
VM = pl.BlockSpec(memory_space=pltpu.VMEM)
HBM = pl.BlockSpec(memory_space=pltpu.HBM)
SCALAR = pl.BlockSpec(memory_space=pltpu.SMEM)


def params(mib=24):
    return pltpu.CompilerParams(vmem_limit_bytes=mib * 1024 * 1024)


def shape(dims, dtype=BF):
    return jax.ShapeDtypeStruct(dims, dtype)


def in_hbm(value):
    return pltpu.with_memory_space_constraint(value, pltpu.HBM)


def own_tiles(where_ref, all_truth_ref, truth_ref, area_ref):
    lane_tiles = LANES // 128
    group, quarter, place = where_ref[0], where_ref[1], where_ref[2]
    cols = pl.ds(pl.multiple_of(quarter * LANES, 128), LANES)
    all_truth = jnp.concatenate(
        [all_truth_ref[:, cols].astype(F32), jnp.zeros((GROUPS * USED + ROWS - USED - C, LANES), F32)], 0
    )
    truth_here = all_truth[:ROWS]
    for g in range(1, GROUPS):
        truth_here = jnp.where(group == g, all_truth[g * USED : g * USED + ROWS], truth_here)
    lane = lax.broadcasted_iota(jnp.int32, (ROWS, LANES), 1)
    row = lax.broadcasted_iota(jnp.int32, (ROWS, LANES), 0)
    position = (place * PTS + quarter * LANES + lane).astype(F32)
    area_here = jnp.cos(math.pi * ((position + 0.5) / NPTS - 0.5))
    area_here = jnp.where((row < USED) & (group * USED + row < C), area_here, 0.0)
    for r in range(ROWS // 8):
        for l in range(lane_tiles):
            tile = (slice(r * 8, (r + 1) * 8), slice(l * 128, (l + 1) * 128))
            truth_ref[r * lane_tiles + l] = truth_here[tile]
            area_ref[r * lane_tiles + l] = area_here[tile]


def forward_kernel(
    where_ref, lat_hbm, w1_hbm, w2_hbm, truth_hbm,
    hid_ref, der_ref, lat_ref, blk_ref, w2t_ref, truth_ref, area_ref,
    w1, w2_ref, all_truth, w2p, field, sems,
):
    halves, spans = 2, PTS // WIDE
    rows = H2 // halves
    w1_in = [
        pltpu.make_async_copy(
            w1_hbm.at[r * rows : (r + 1) * rows], w1.at[r * rows : (r + 1) * rows], sems.at[r]
        )
        for r in range(halves)
    ]
    lat_in = [
        pltpu.make_async_copy(
            lat_hbm.at[0, :, n * WIDE : (n + 1) * WIDE],
            lat_ref.at[:, n * WIDE : (n + 1) * WIDE],
            sems.at[halves + n],
        )
        for n in range(spans)
    ]
    w2_in = pltpu.make_async_copy(w2_hbm, w2_ref, sems.at[halves + spans])
    truth_in = pltpu.make_async_copy(truth_hbm, all_truth, sems.at[halves + spans + 1])
    for copy in [w2_in, truth_in, w1_in[0], lat_in[0]] + w1_in[1:] + lat_in[1:]:
        copy.start()
    w2_in.wait()
    w2 = jnp.concatenate([w2_ref[...].astype(F32), jnp.zeros((1, H2), F32)], 0)
    gap = jnp.zeros((ROWS - USED, H2), F32)
    parts = []
    for g in range(GROUPS):
        parts += [w2[g * USED : (g + 1) * USED], gap]
    padded = jnp.concatenate(parts, 0)
    w2p[...] = padded.astype(BF)
    w2t_ref[...] = (0.5 * jnp.concatenate([padded, jnp.zeros((128 - PAD, H2), F32)], 0)).T.astype(BF)

    def decode(n):
        cols = slice(n * WIDE, (n + 1) * WIDE)
        field[:, cols] = jnp.dot(w2p[...], hid_ref[:, cols], preferred_element_type=F32)

    def gate(pre, here, cols):
        half = 0.5 * pre
        t = jnp.tanh(half)
        twice = 1.0 + t
        act = half * twice
        hid_ref[here, cols] = act.astype(BF)
        der_ref[here, cols] = (twice + act * (1.0 - t)).astype(BF)

    held = None
    for n in range(spans):
        if n == 0:
            lat_in[0].wait()
        if n == 1:
            truth_in.wait()
            for copy in lat_in[1:]:
                copy.wait()
            own_tiles(where_ref, all_truth, truth_ref, area_ref)
        cols = slice(n * WIDE, (n + 1) * WIDE)
        for r in range(0, H2, 128):
            if n == 0 and r % rows == 0:
                w1_in[r // rows].wait()
            here = slice(r, r + 128)
            pre = jnp.dot(w1[here, :], lat_ref[:, cols], preferred_element_type=F32)
            if held is not None:
                gate(*held)
            held = (pre, here, cols)
        if n > 0:
            decode(n - 1)
    gate(*held)
    decode(spans - 1)
    for g in range(GROUPS):
        for q in range(PTS // LANES):
            blk_ref[q * GROUPS + g] = field[
                g * ROWS : (g + 1) * ROWS, q * LANES : (q + 1) * LANES
            ].astype(BF)


def forward(where, latent, w_first, w_second, truth):
    spots = ROWS // 8 * (LANES // 128)
    return pl.pallas_call(
        forward_kernel,
        in_specs=[SCALAR, HBM, HBM, HBM, HBM],
        out_specs=[VM] * 7,
        out_shape=[
            shape((H2, PTS)),
            shape((H2, PTS)),
            shape((H, PTS)),
            shape((16, ROWS, LANES)),
            shape((H2, 128)),
            shape((spots, 8, 128), F32),
            shape((spots, 8, 128), F32),
        ],
        scratch_shapes=[
            pltpu.VMEM((H2, H), BF),
            pltpu.VMEM((C, H2), BF),
            pltpu.VMEM((C, PTS), BF),
            pltpu.VMEM((PAD, H2), BF),
            pltpu.VMEM((PAD, PTS), F32),
            pltpu.SemaphoreType.DMA((4 + PTS // WIDE,)),
        ],
        compiler_params=params(12),
        name="forward",
    )(where, in_hbm(latent), in_hbm(w_first), in_hbm(w_second), in_hbm(truth))


def pair_kernel(fields_ref, truth_ref, area_ref, out_ref, values, grads):
    lane_tiles = LANES // 128
    for m in range(MEMBERS):
        block = fields_ref[m].astype(F32)
        for r in range(ROWS // 8):
            for l in range(lane_tiles):
                values[r * lane_tiles + l, m] = block[
                    r * 8 : (r + 1) * 8, l * 128 : (l + 1) * 128
                ]

    def spot(index, losses):
        v = [values[index, m] for m in range(MEMBERS)]
        truth = truth_ref[index]
        area = area_ref[index]
        value = [None] * MEMBERS
        slope = [None] * MEMBERS

        def add(store, m, term):
            store[m] = term if store[m] is None else store[m] + term

        for m in range(MEMBERS):
            for k in range(m + 1, MEMBERS):
                d = v[m] - v[k]
                square = d * d + EPS
                inverse = lax.rsqrt(square)
                s = square * inverse
                t = d * inverse
                add(value, m, s)
                add(value, k, s)
                add(slope, m, t)
                slope[k] = -t if slope[k] is None else slope[k] - t
        new = []
        for m in range(MEMBERS):
            gap = v[m] - truth
            square = gap * gap + EPS
            inverse = lax.rsqrt(square)
            grads[index, m] = area * (
                gap * inverse * (1.0 / MEMBERS)
                - slope[m] * (1.0 / (MEMBERS * (MEMBERS - 1)))
            )
            new.append(area * (square * inverse - value[m] * (1.0 / (2.0 * (MEMBERS - 1)))))
        return [a + b for a, b in zip(losses, new)]

    zero = [jnp.zeros((8, 128), F32) for _ in range(MEMBERS)]
    row = lax.broadcasted_iota(jnp.int32, (8, 128), 0)
    last = ROWS // 8 - 1
    for l in range(lane_tiles):
        losses = lax.fori_loop(
            0, ROWS // 8, lambda r, carry: spot(r * lane_tiles + l, carry), zero
        )
        for m in range(MEMBERS):
            loss = jnp.sum(losses[m], axis=0, keepdims=True)
            high = loss.astype(BF).astype(F32)
            low = loss - high
            at = last * lane_tiles + l
            kept = grads[at, m]
            grads[at, m] = jnp.where(
                row == HI - 8 * last, high, jnp.where(row == LO - 8 * last, low, kept)
            )
    for m in range(MEMBERS):
        out_ref[m] = jnp.concatenate(
            [
                jnp.concatenate([grads[r * lane_tiles + l, m] for l in range(lane_tiles)], 1)
                for r in range(ROWS // 8)
            ],
            0,
        ).astype(BF)


def pairs(fields, truth, area):
    spots = ROWS // 8 * (LANES // 128)
    return pl.pallas_call(
        pair_kernel,
        out_shape=shape((16, ROWS, LANES)),
        in_specs=[VM] * 3,
        out_specs=VM,
        scratch_shapes=[
            pltpu.VMEM((spots, MEMBERS, 8, 128), F32),
            pltpu.VMEM((spots, MEMBERS, 8, 128), F32),
        ],
        compiler_params=params(6),
        name="pairs",
    )(fields, truth, area)


def arrange(rows):
    out = []
    for y in range(4):
        for x in range(4):
            pick = [rows[x * 64 + zh * 32 + y * 8 : x * 64 + zh * 32 + y * 8 + 8] for zh in range(2)]
            out.append(jnp.concatenate(pick, 0))
    return out


def half_of_first(bp_ref, lat_ref, half, out_ref):
    lat = lat_ref[pl.ds(pl.multiple_of(half * (H // 2), H // 2), H // 2), :]
    for z in range(4):
        part = lax.dot_general(
            bp_ref[z * 256 : (z + 1) * 256, :], lat, NT, preferred_element_type=F32
        )
        for e, piece in enumerate(arrange(part)):
            out_ref[e, z * 16 : (z + 1) * 16, :] = piece.astype(out_ref.dtype)


def back_kernel(core_ref, blk_ref, der_ref, lat_ref, w2t_ref, bp_ref, send_ref, low_ref):
    for q in range(PTS // LANES):
        parts = [blk_ref[q * GROUPS + g].astype(F32) for g in range(GROUPS)]
        parts.append(jnp.zeros((128 - PAD, LANES), F32))
        low_ref[:, q * LANES : (q + 1) * LANES] = jnp.concatenate(parts, 0).astype(BF)
    for n in range(PTS // WIDE):
        cols = slice(n * WIDE, (n + 1) * WIDE)
        back = jnp.dot(w2t_ref[...], low_ref[:, cols], preferred_element_type=F32)
        bp_ref[:, cols] = (back * der_ref[:, cols].astype(F32)).astype(BF)
    half_of_first(bp_ref, lat_ref, 1 - core_ref[0], send_ref)


def backward(core, blocks, deriv, latent, w2t):
    return pl.pallas_call(
        back_kernel,
        in_specs=[SCALAR, VM, VM, VM, VM],
        out_specs=[VM] * 3,
        out_shape=[shape((H2, PTS)), shape((16, 64, H // 2)), shape((128, PTS))],
        compiler_params=params(12),
        name="backward",
    )(core, blocks, deriv, latent, w2t)


def own_kernel(core_ref, bp_ref, lat_ref, out_ref):
    half_of_first(bp_ref, lat_ref, core_ref[0], out_ref)


def own_half(core, bp, latent):
    return pl.pallas_call(
        own_kernel,
        in_specs=[SCALAR, VM, VM],
        out_specs=VM,
        out_shape=shape((16, 64, H // 2), F32),
        compiler_params=params(12),
        cost_estimate=pl.CostEstimate(
            flops=2 * H2 * (H // 2) * PTS, bytes_accessed=8 * 1024 * 1024, transcendentals=0
        ),
        name="own_half",
    )(core, bp, latent)


def emit_kernel(low_ref, grad_ref):
    for g in range(GROUPS):
        used = min(USED, C - g * USED)
        part = low_ref[g * ROWS : (g + 1) * ROWS, :].astype(F32)
        grad_ref[g * USED : g * USED + used] = part[:used].reshape(used, 1, PTS)


def emit(low):
    return pl.pallas_call(
        emit_kernel,
        in_specs=[VM],
        out_specs=VM,
        out_shape=shape((C, 1, PTS), F32),
        compiler_params=params(6),
        cost_estimate=pl.CostEstimate(flops=0, bytes_accessed=PTS, transcendentals=0),
        name="emit",
    )(low)


def second_kernel(core_ref, low_ref, hid_ref, keep_ref, send_ref, second):
    half = H2 // 2
    second[...] = lax.dot_general(low_ref[...], hid_ref[...], NT, preferred_element_type=F32)[:PAD]
    row = lax.broadcasted_iota(jnp.int32, (8, LANES), 0)
    total = jnp.zeros((1, LANES), F32)
    for g in range(GROUPS):
        block = low_ref[g * ROWS : (g + 1) * ROWS, :].astype(F32)
        for q in range(PTS // LANES):
            cols = slice(q * LANES, (q + 1) * LANES)
            total += block[HI : HI + 1, cols] + block[LO : LO + 1, cols]
    high = total.astype(BF).astype(F32)
    top = ROWS - 8
    second[top:ROWS, :LANES] = jnp.where(
        row == HI - top,
        high,
        jnp.where(row == LO - top, total - high, second[top:ROWS, :LANES]),
    )
    keep_ref[...] = second[:, pl.ds(pl.multiple_of(core_ref[0] * half, half), half)]
    send_ref[...] = second[:, pl.ds(pl.multiple_of((1 - core_ref[0]) * half, half), half)].astype(BF)


def second_halves(core, low, hidden):
    return pl.pallas_call(
        second_kernel,
        in_specs=[SCALAR, VM, VM],
        out_specs=[VM] * 2,
        out_shape=[shape((PAD, H2 // 2), F32), shape((PAD, H2 // 2))],
        scratch_shapes=[pltpu.VMEM((PAD, H2), F32)],
        compiler_params=params(12),
        name="second",
    )(core, low, hidden)


def total_of(parts_ref, which):
    total = parts_ref[which[0]].astype(F32)
    for e in which[1:]:
        total += parts_ref[e].astype(F32)
    return total


def sum_chips_kernel(parts_ref, out_ref):
    total = total_of(parts_ref, range(16))
    for z in range(8):
        for c in range(2):
            at = z * 8 + c * 4
            out_ref[c * 8 + z % 2 * 4 + z // 2] = total[at : at + 4].astype(BF)


def sum_chips(parts):
    return pl.pallas_call(
        sum_chips_kernel,
        in_specs=[VM],
        out_specs=VM,
        out_shape=shape((16, 4, H // 2)),
        compiler_params=params(6),
        cost_estimate=pl.CostEstimate(flops=FLOPS, bytes_accessed=parts.size * 2, transcendentals=0),
        name="sum_chips",
    )(parts)


def sum_last_kernel(parts_ref, out_ref):
    half = H // 2
    for c in range(2):
        total = total_of(parts_ref, range(c * 8, c * 8 + 8))
        out_ref[:, c * half : (c + 1) * half] = total * (1.0 / math.sqrt(MEMBERS * NPTS))


def sum_last(parts):
    return pl.pallas_call(
        sum_last_kernel,
        in_specs=[VM],
        out_specs=VM,
        out_shape=shape((4, H), F32),
        compiler_params=params(6),
        cost_estimate=pl.CostEstimate(flops=FLOPS, bytes_accessed=parts.size * 2, transcendentals=0),
        name="sum_last",
    )(parts)


def finish_kernel(core_ref, mine_ref, other_ref, second_ref, loss_ref):
    half = H // 2
    first_core = core_ref[0] == 0
    mine, other = mine_ref[...].astype(F32), other_ref[...].astype(F32)
    left, right = jnp.where(first_core, mine, other), jnp.where(first_core, other, mine)
    loss = left[HI : HI + 1, :LANES] + left[LO : LO + 1, :LANES]
    loss_ref[...] = jnp.sum(loss, axis=1, keepdims=True) / NPTS
    scale = MEMBERS / math.sqrt(NPTS)
    for g in range(GROUPS):
        used = min(USED, C - g * USED)
        for cols, part in ((slice(0, half), left), (slice(half, H2), right)):
            rows = part[g * ROWS : g * ROWS + used] * scale
            second_ref[g * USED : g * USED + used, :, cols] = rows.reshape(used, 1, half)


def finish(core, mine, other):
    return pl.pallas_call(
        finish_kernel,
        in_specs=[SCALAR, VM, VM],
        out_specs=[VM] * 2,
        out_shape=[shape((C, 1, H2), F32), shape((1, 1), F32)],
        compiler_params=params(6),
        cost_estimate=pl.CostEstimate(flops=0, bytes_accessed=PTS, transcendentals=0),
        name="finish",
    )(core, mine, other)


def swap(value, axis, by):
    size = lax.axis_size(axis)
    return lax.ppermute(value, axis, [(i, i ^ by) for i in range(size)])


def cross(value, h, y):
    pairs = []
    for zh in range(2):
        for k in range(4):
            for c in range(2):
                mate = (k + (1 if k % 2 == c else 3)) % 4 if y else k
                pairs.append(((zh * 4 + k) * 2 + c, ((zh ^ h) * 4 + mate) * 2 + c))
    return lax.ppermute(value, ("zh", "y", "c"), pairs)


def packed(total):
    row = lax.broadcasted_iota(jnp.int32, total.shape, 0)
    loss = total[HI : HI + 1] + total[LO : LO + 1]
    high = lax.reduce_precision(loss, 8, 7)
    return jnp.where(row == HI, high, jnp.where(row == LO, loss - high, total)).astype(BF)


def on_device(latent, truth, w_first, w_second):
    core = lax.axis_index("c").astype(jnp.int32)
    group, quarter = lax.axis_index("zl"), lax.axis_index("x")
    place = (lax.axis_index("zh") * 4 + lax.axis_index("y")) * 2 + lax.axis_index("c")
    where = jnp.stack([group, quarter, place]).astype(jnp.int32)
    latent, where, core = lax.optimization_barrier((latent, where, core[None]))

    hidden, deriv, kept_latent, blocks, w2t, truth_here, area = forward(
        where, latent, w_first, w_second, truth
    )

    gathered = lax.all_to_all(blocks, ("x", "zl"), 0, 0, tiled=True)
    grads = pairs(gathered, truth_here, area)
    grads = lax.all_to_all(grads, ("x", "zl"), 0, 0, tiled=True)

    bp, send, low = backward(core, grads, deriv, kept_latent, w2t)
    arrived = swap(send, "c", 1)
    keep2, send2 = second_halves(core, low, hidden)
    arrived2 = swap(send2, "c", 1)
    own = own_half(core, bp, kept_latent)
    first = (own + arrived.astype(F32)).astype(BF)
    total = packed(keep2 + arrived2.astype(F32))
    first, total, low = lax.optimization_barrier((first, total, low))

    field_grad = emit(low)
    near, far, both = (cross(total, h, y).astype(F32) for h, y in ((0, 1), (1, 0), (1, 1)))
    total = packed((total.astype(F32) + both) + (near + far))
    first = lax.all_to_all(first, ("y", "x"), 0, 0, tiled=True)
    first = sum_chips(first)
    first, total, field_grad = lax.optimization_barrier((first, total, field_grad))

    total = packed(total.astype(F32) + swap(total, "y", 2).astype(F32))
    second_out, loss = finish(core, total, swap(total, "c", 1))
    first = lax.all_to_all(first, ("c", "zh", "zl"), 0, 0, tiled=True)
    first, second_out, loss = lax.optimization_barrier((first, second_out, loss))
    return loss[0], field_grad.transpose(1, 0, 2), sum_last(first), second_out.transpose(1, 0, 2)


def solution(mesh):
    fine = Mesh(mesh.devices.reshape(4, 4, 2, 4, 2), ("zl", "x", "zh", "y", "c"))
    ens, space = ("zl", "x"), ("zh", "y", "c")
    in_specs = (P(ens, None, space), P(None, space), P(), P())
    out_specs = (P(ens), P(ens, None, space), P(ens + space, None), P(ens, None, None))
    return jax.shard_map(
        on_device, mesh=fine, in_specs=in_specs, out_specs=out_specs, check_vma=False
    )
```

```python
import functools
import math

import jax
import jax.numpy as jnp
from jax import lax
from jax.experimental import pallas as pl
from jax.experimental.pallas import tpu as pltpu
from jax.sharding import Mesh
from jax.sharding import PartitionSpec as P

BF = jnp.bfloat16
F32 = jnp.float32
EPS = 0.01
C, H, H2 = 83, 1024, 1024
PTS = 1536
NPTS = 24576
MEMBERS = 16
GROUPS, USED, ROWS, LANES = 4, 21, 24, 384
PAD = GROUPS * ROWS
WIDE = 512
HI, LO = 21, 22
FLOPS = 20_000_000_000
NT = (((1,), (1,)), ((), ()))
VM = pl.BlockSpec(memory_space=pltpu.VMEM)
HBM = pl.BlockSpec(memory_space=pltpu.HBM)
SCALAR = pl.BlockSpec(memory_space=pltpu.SMEM)


def params(mib=24):
    return pltpu.CompilerParams(vmem_limit_bytes=mib * 1024 * 1024)


def shape(dims, dtype=BF):
    return jax.ShapeDtypeStruct(dims, dtype)


def in_hbm(value):
    return pltpu.with_memory_space_constraint(value, pltpu.HBM)


def own_tiles(where_ref, all_truth_ref, truth_ref, area_ref):
    lane_tiles = LANES // 128
    group, quarter, place = where_ref[0], where_ref[1], where_ref[2]
    cols = pl.ds(pl.multiple_of(quarter * LANES, 128), LANES)
    all_truth = jnp.concatenate(
        [all_truth_ref[:, cols].astype(F32), jnp.zeros((GROUPS * USED + ROWS - USED - C, LANES), F32)], 0
    )
    truth_here = all_truth[:ROWS]
    for g in range(1, GROUPS):
        truth_here = jnp.where(group == g, all_truth[g * USED : g * USED + ROWS], truth_here)
    lane = lax.broadcasted_iota(jnp.int32, (ROWS, LANES), 1)
    row = lax.broadcasted_iota(jnp.int32, (ROWS, LANES), 0)
    position = (place * PTS + quarter * LANES + lane).astype(F32)
    area_here = jnp.cos(math.pi * ((position + 0.5) / NPTS - 0.5))
    area_here = jnp.where((row < USED) & (group * USED + row < C), area_here, 0.0)
    for r in range(ROWS // 8):
        for l in range(lane_tiles):
            tile = (slice(r * 8, (r + 1) * 8), slice(l * 128, (l + 1) * 128))
            truth_ref[r * lane_tiles + l] = truth_here[tile]
            area_ref[r * lane_tiles + l] = area_here[tile]


def forward_kernel(
    where_ref, lat_hbm, w1_hbm, w2_hbm, truth_hbm,
    hid_ref, der_ref, lat_ref, blk_ref, w2t_ref, truth_ref, area_ref,
    w1, w2_ref, all_truth, w2p, field, sems,
):
    halves, spans = 2, PTS // WIDE
    rows = H2 // halves
    w1_in = [
        pltpu.make_async_copy(
            w1_hbm.at[r * rows : (r + 1) * rows], w1.at[r * rows : (r + 1) * rows], sems.at[r]
        )
        for r in range(halves)
    ]
    lat_in = [
        pltpu.make_async_copy(
            lat_hbm.at[0, :, n * WIDE : (n + 1) * WIDE],
            lat_ref.at[:, n * WIDE : (n + 1) * WIDE],
            sems.at[halves + n],
        )
        for n in range(spans)
    ]
    w2_in = pltpu.make_async_copy(w2_hbm, w2_ref, sems.at[halves + spans])
    truth_in = pltpu.make_async_copy(truth_hbm, all_truth, sems.at[halves + spans + 1])
    for copy in [w2_in, truth_in, w1_in[0], lat_in[0]] + w1_in[1:] + lat_in[1:]:
        copy.start()
    w2_in.wait()
    w2 = jnp.concatenate([w2_ref[...].astype(F32), jnp.zeros((1, H2), F32)], 0)
    gap = jnp.zeros((ROWS - USED, H2), F32)
    parts = []
    for g in range(GROUPS):
        parts += [w2[g * USED : (g + 1) * USED], gap]
    padded = jnp.concatenate(parts, 0)
    w2p[...] = padded.astype(BF)
    w2t_ref[...] = (0.5 * jnp.concatenate([padded, jnp.zeros((128 - PAD, H2), F32)], 0)).T.astype(BF)

    def decode(n):
        cols = slice(n * WIDE, (n + 1) * WIDE)
        field[:, cols] = jnp.dot(w2p[...], hid_ref[:, cols], preferred_element_type=F32)

    def gate(pre, here, cols):
        half = 0.5 * pre
        t = jnp.tanh(half)
        twice = 1.0 + t
        act = half * twice
        hid_ref[here, cols] = act.astype(BF)
        der_ref[here, cols] = (twice + act * (1.0 - t)).astype(BF)

    held = None
    for n in range(spans):
        if n == 0:
            lat_in[0].wait()
        if n == 1:
            truth_in.wait()
            for copy in lat_in[1:]:
                copy.wait()
            own_tiles(where_ref, all_truth, truth_ref, area_ref)
        cols = slice(n * WIDE, (n + 1) * WIDE)
        for r in range(0, H2, 128):
            if n == 0 and r % rows == 0:
                w1_in[r // rows].wait()
            here = slice(r, r + 128)
            pre = jnp.dot(w1[here, :], lat_ref[:, cols], preferred_element_type=F32)
            if held is not None:
                gate(*held)
            held = (pre, here, cols)
        if n > 0:
            decode(n - 1)
    gate(*held)
    decode(spans - 1)
    for g in range(GROUPS):
        for q in range(PTS // LANES):
            blk_ref[q * GROUPS + g] = field[
                g * ROWS : (g + 1) * ROWS, q * LANES : (q + 1) * LANES
            ].astype(BF)


def forward(where, latent, w_first, w_second, truth):
    spots = ROWS // 8 * (LANES // 128)
    return pl.pallas_call(
        forward_kernel,
        in_specs=[SCALAR, HBM, HBM, HBM, HBM],
        out_specs=[VM] * 7,
        out_shape=[
            shape((H2, PTS)),
            shape((H2, PTS)),
            shape((H, PTS)),
            shape((16, ROWS, LANES)),
            shape((H2, 128)),
            shape((spots, 8, 128), F32),
            shape((spots, 8, 128), F32),
        ],
        scratch_shapes=[
            pltpu.VMEM((H2, H), BF),
            pltpu.VMEM((C, H2), BF),
            pltpu.VMEM((C, PTS), BF),
            pltpu.VMEM((PAD, H2), BF),
            pltpu.VMEM((PAD, PTS), F32),
            pltpu.SemaphoreType.DMA((4 + PTS // WIDE,)),
        ],
        compiler_params=params(12),
        name="forward",
    )(where, in_hbm(latent), in_hbm(w_first), in_hbm(w_second), in_hbm(truth))


def pair_kernel(fields_ref, truth_ref, area_ref, out_ref, values, grads):
    lane_tiles = LANES // 128
    for m in range(MEMBERS):
        block = fields_ref[m].astype(F32)
        for r in range(ROWS // 8):
            for l in range(lane_tiles):
                values[r * lane_tiles + l, m] = block[
                    r * 8 : (r + 1) * 8, l * 128 : (l + 1) * 128
                ]

    def spot(index, losses):
        v = [values[index, m] for m in range(MEMBERS)]
        truth = truth_ref[index]
        area = area_ref[index]
        value = [None] * MEMBERS
        slope = [None] * MEMBERS

        def add(store, m, term):
            store[m] = term if store[m] is None else store[m] + term

        for m in range(MEMBERS):
            for k in range(m + 1, MEMBERS):
                d = v[m] - v[k]
                square = d * d + EPS
                inverse = lax.rsqrt(square)
                s = square * inverse
                t = d * inverse
                add(value, m, s)
                add(value, k, s)
                add(slope, m, t)
                slope[k] = -t if slope[k] is None else slope[k] - t
        new = []
        for m in range(MEMBERS):
            gap = v[m] - truth
            square = gap * gap + EPS
            inverse = lax.rsqrt(square)
            grads[index, m] = area * (
                gap * inverse * (1.0 / MEMBERS)
                - slope[m] * (1.0 / (MEMBERS * (MEMBERS - 1)))
            )
            new.append(area * (square * inverse - value[m] * (1.0 / (2.0 * (MEMBERS - 1)))))
        return [a + b for a, b in zip(losses, new)]

    zero = [jnp.zeros((8, 128), F32) for _ in range(MEMBERS)]
    row = lax.broadcasted_iota(jnp.int32, (8, 128), 0)
    last = ROWS // 8 - 1
    for l in range(lane_tiles):
        losses = zero
        for r in range(ROWS // 8):
            losses = spot(r * lane_tiles + l, losses)
        for m in range(MEMBERS):
            loss = jnp.sum(losses[m], axis=0, keepdims=True)
            high = loss.astype(BF).astype(F32)
            low = loss - high
            at = last * lane_tiles + l
            kept = grads[at, m]
            grads[at, m] = jnp.where(
                row == HI - 8 * last, high, jnp.where(row == LO - 8 * last, low, kept)
            )
    for m in range(MEMBERS):
        out_ref[m] = jnp.concatenate(
            [
                jnp.concatenate([grads[r * lane_tiles + l, m] for l in range(lane_tiles)], 1)
                for r in range(ROWS // 8)
            ],
            0,
        ).astype(BF)


def pairs(fields, truth, area):
    spots = ROWS // 8 * (LANES // 128)
    return pl.pallas_call(
        pair_kernel,
        out_shape=shape((16, ROWS, LANES)),
        in_specs=[VM] * 3,
        out_specs=VM,
        scratch_shapes=[
            pltpu.VMEM((spots, MEMBERS, 8, 128), F32),
            pltpu.VMEM((spots, MEMBERS, 8, 128), F32),
        ],
        compiler_params=params(6),
        name="pairs",
    )(fields, truth, area)


def arrange(rows):
    out = []
    for y in range(4):
        for x in range(4):
            pick = [rows[x * 64 + zh * 32 + y * 8 : x * 64 + zh * 32 + y * 8 + 8] for zh in range(2)]
            out.append(jnp.concatenate(pick, 0))
    return out


def half_of_first(bp_ref, lat_ref, half, out_ref):
    lat = lat_ref[pl.ds(pl.multiple_of(half * (H // 2), H // 2), H // 2), :]
    for z in range(4):
        part = lax.dot_general(
            bp_ref[z * 256 : (z + 1) * 256, :], lat, NT, preferred_element_type=F32
        )
        for e, piece in enumerate(arrange(part)):
            out_ref[e, z * 16 : (z + 1) * 16, :] = piece.astype(out_ref.dtype)


def back_kernel(core_ref, blk_ref, der_ref, lat_ref, w2t_ref, bp_ref, send_ref, low_ref):
    for q in range(PTS // LANES):
        parts = [blk_ref[q * GROUPS + g].astype(F32) for g in range(GROUPS)]
        parts.append(jnp.zeros((128 - PAD, LANES), F32))
        low_ref[:, q * LANES : (q + 1) * LANES] = jnp.concatenate(parts, 0).astype(BF)
    for n in range(PTS // WIDE):
        cols = slice(n * WIDE, (n + 1) * WIDE)
        back = jnp.dot(w2t_ref[...], low_ref[:, cols], preferred_element_type=F32)
        bp_ref[:, cols] = (back * der_ref[:, cols].astype(F32)).astype(BF)
    half_of_first(bp_ref, lat_ref, 1 - core_ref[0], send_ref)


def backward(core, blocks, deriv, latent, w2t):
    return pl.pallas_call(
        back_kernel,
        in_specs=[SCALAR, VM, VM, VM, VM],
        out_specs=[VM] * 3,
        out_shape=[shape((H2, PTS)), shape((16, 64, H // 2)), shape((128, PTS))],
        compiler_params=params(12),
        name="backward",
    )(core, blocks, deriv, latent, w2t)


def own_kernel(core_ref, bp_ref, lat_ref, out_ref):
    half_of_first(bp_ref, lat_ref, core_ref[0], out_ref)


def own_half(core, bp, latent):
    return pl.pallas_call(
        own_kernel,
        in_specs=[SCALAR, VM, VM],
        out_specs=VM,
        out_shape=shape((16, 64, H // 2), F32),
        compiler_params=params(12),
        cost_estimate=pl.CostEstimate(
            flops=2 * H2 * (H // 2) * PTS, bytes_accessed=8 * 1024 * 1024, transcendentals=0
        ),
        name="own_half",
    )(core, bp, latent)


def emit_kernel(low_ref, grad_ref):
    for g in range(GROUPS):
        used = min(USED, C - g * USED)
        part = low_ref[g * ROWS : (g + 1) * ROWS, :].astype(F32)
        grad_ref[g * USED : g * USED + used] = part[:used].reshape(used, 1, PTS)


def emit(low):
    return pl.pallas_call(
        emit_kernel,
        in_specs=[VM],
        out_specs=VM,
        out_shape=shape((C, 1, PTS), F32),
        compiler_params=params(6),
        cost_estimate=pl.CostEstimate(flops=0, bytes_accessed=PTS, transcendentals=0),
        name="emit",
    )(low)


def second_kernel(core_ref, low_ref, hid_ref, keep_ref, send_ref, second):
    half = H2 // 2
    second[...] = lax.dot_general(low_ref[...], hid_ref[...], NT, preferred_element_type=F32)[:PAD]
    row = lax.broadcasted_iota(jnp.int32, (8, LANES), 0)
    total = jnp.zeros((1, LANES), F32)
    for g in range(GROUPS):
        block = low_ref[g * ROWS : (g + 1) * ROWS, :].astype(F32)
        for q in range(PTS // LANES):
            cols = slice(q * LANES, (q + 1) * LANES)
            total += block[HI : HI + 1, cols] + block[LO : LO + 1, cols]
    high = total.astype(BF).astype(F32)
    top = ROWS - 8
    second[top:ROWS, :LANES] = jnp.where(
        row == HI - top,
        high,
        jnp.where(row == LO - top, total - high, second[top:ROWS, :LANES]),
    )
    keep_ref[...] = second[:, pl.ds(pl.multiple_of(core_ref[0] * half, half), half)]
    send_ref[...] = second[:, pl.ds(pl.multiple_of((1 - core_ref[0]) * half, half), half)].astype(BF)


def second_halves(core, low, hidden):
    return pl.pallas_call(
        second_kernel,
        in_specs=[SCALAR, VM, VM],
        out_specs=[VM] * 2,
        out_shape=[shape((PAD, H2 // 2), F32), shape((PAD, H2 // 2))],
        scratch_shapes=[pltpu.VMEM((PAD, H2), F32)],
        compiler_params=params(12),
        name="second",
    )(core, low, hidden)


def total_of(parts_ref, which):
    total = parts_ref[which[0]].astype(F32)
    for e in which[1:]:
        total += parts_ref[e].astype(F32)
    return total


def sum_chips_kernel(parts_ref, out_ref):
    total = total_of(parts_ref, range(16))
    for z in range(8):
        for c in range(2):
            at = z * 8 + c * 4
            out_ref[c * 8 + z % 2 * 4 + z // 2] = total[at : at + 4].astype(BF)


def sum_chips(parts):
    return pl.pallas_call(
        sum_chips_kernel,
        in_specs=[VM],
        out_specs=VM,
        out_shape=shape((16, 4, H // 2)),
        compiler_params=params(6),
        cost_estimate=pl.CostEstimate(flops=FLOPS, bytes_accessed=parts.size * 2, transcendentals=0),
        name="sum_chips",
    )(parts)


def sum_last_kernel(parts_ref, out_ref):
    half = H // 2
    for c in range(2):
        total = total_of(parts_ref, range(c * 8, c * 8 + 8))
        out_ref[:, c * half : (c + 1) * half] = total * (1.0 / math.sqrt(MEMBERS * NPTS))


def sum_last(parts):
    return pl.pallas_call(
        sum_last_kernel,
        in_specs=[VM],
        out_specs=VM,
        out_shape=shape((4, H), F32),
        compiler_params=params(6),
        cost_estimate=pl.CostEstimate(flops=FLOPS, bytes_accessed=parts.size * 2, transcendentals=0),
        name="sum_last",
    )(parts)


def finish_kernel(core_ref, mine_ref, other_ref, second_ref, loss_ref):
    half = H // 2
    first_core = core_ref[0] == 0
    mine, other = mine_ref[...].astype(F32), other_ref[...].astype(F32)
    left, right = jnp.where(first_core, mine, other), jnp.where(first_core, other, mine)
    loss = left[HI : HI + 1, :LANES] + left[LO : LO + 1, :LANES]
    loss_ref[...] = jnp.sum(loss, axis=1, keepdims=True) / NPTS
    scale = MEMBERS / math.sqrt(NPTS)
    for g in range(GROUPS):
        used = min(USED, C - g * USED)
        for cols, part in ((slice(0, half), left), (slice(half, H2), right)):
            rows = part[g * ROWS : g * ROWS + used] * scale
            second_ref[g * USED : g * USED + used, :, cols] = rows.reshape(used, 1, half)


def finish(core, mine, other):
    return pl.pallas_call(
        finish_kernel,
        in_specs=[SCALAR, VM, VM],
        out_specs=[VM] * 2,
        out_shape=[shape((C, 1, H2), F32), shape((1, 1), F32)],
        compiler_params=params(6),
        cost_estimate=pl.CostEstimate(flops=0, bytes_accessed=PTS, transcendentals=0),
        name="finish",
    )(core, mine, other)


def swap(value, axis, by):
    size = lax.axis_size(axis)
    return lax.ppermute(value, axis, [(i, i ^ by) for i in range(size)])


def cross(value, h, y):
    pairs = []
    for zh in range(2):
        for k in range(4):
            for c in range(2):
                mate = (k + (1 if k % 2 == c else 3)) % 4 if y else k
                pairs.append(((zh * 4 + k) * 2 + c, ((zh ^ h) * 4 + mate) * 2 + c))
    return lax.ppermute(value, ("zh", "y", "c"), pairs)


def packed(total):
    row = lax.broadcasted_iota(jnp.int32, total.shape, 0)
    loss = total[HI : HI + 1] + total[LO : LO + 1]
    high = lax.reduce_precision(loss, 8, 7)
    return jnp.where(row == HI, high, jnp.where(row == LO, loss - high, total)).astype(BF)


def on_device(latent, truth, w_first, w_second):
    core = lax.axis_index("c").astype(jnp.int32)
    group, quarter = lax.axis_index("zl"), lax.axis_index("x")
    place = (lax.axis_index("zh") * 4 + lax.axis_index("y")) * 2 + lax.axis_index("c")
    where = jnp.stack([group, quarter, place]).astype(jnp.int32)
    latent, where, core = lax.optimization_barrier((latent, where, core[None]))

    hidden, deriv, kept_latent, blocks, w2t, truth_here, area = forward(
        where, latent, w_first, w_second, truth
    )

    gathered = lax.all_to_all(blocks, ("x", "zl"), 0, 0, tiled=True)
    grads = pairs(gathered, truth_here, area)
    grads = lax.all_to_all(grads, ("x", "zl"), 0, 0, tiled=True)

    bp, send, low = backward(core, grads, deriv, kept_latent, w2t)
    arrived = swap(send, "c", 1)
    keep2, send2 = second_halves(core, low, hidden)
    arrived2 = swap(send2, "c", 1)
    own = own_half(core, bp, kept_latent)
    first = (own + arrived.astype(F32)).astype(BF)
    total = packed(keep2 + arrived2.astype(F32))
    first, total, low = lax.optimization_barrier((first, total, low))

    field_grad = emit(low)
    near, far, both = (cross(total, h, y).astype(F32) for h, y in ((0, 1), (1, 0), (1, 1)))
    total = packed((total.astype(F32) + both) + (near + far))
    first = lax.all_to_all(first, ("y", "x"), 0, 0, tiled=True)
    first = sum_chips(first)
    first, total, field_grad = lax.optimization_barrier((first, total, field_grad))

    total = packed(total.astype(F32) + swap(total, "y", 2).astype(F32))
    second_out, loss = finish(core, total, swap(total, "c", 1))
    first = lax.all_to_all(first, ("c", "zh", "zl"), 0, 0, tiled=True)
    first, second_out, loss = lax.optimization_barrier((first, second_out, loss))
    return loss[0], field_grad.transpose(1, 0, 2), sum_last(first), second_out.transpose(1, 0, 2)


def solution(mesh):
    fine = Mesh(mesh.devices.reshape(4, 4, 2, 4, 2), ("zl", "x", "zh", "y", "c"))
    ens, space = ("zl", "x"), ("zh", "y", "c")
    in_specs = (P(ens, None, space), P(None, space), P(), P())
    out_specs = (P(ens), P(ens, None, space), P(ens + space, None), P(ens, None, None))
    return jax.shard_map(
        on_device, mesh=fine, in_specs=in_specs, out_specs=out_specs, check_vma=False
    )
```
